256 devices in a mesh: freq: 16 (over x, y_hi, core), src: 16 (over y_lo, z).
Axes of the slice: x: 4, y: 4 (y_hi: 2, y_lo: 2; y = y_hi * 2 + y_lo), z: 8, core: 2. Of those that a mesh axis runs over, the one named last changes fastest.
Arguments:
- spectra: bfloat16 [192, 2, 256, 8192], P('freq', None, None, 'src'), may hold values from -6 to 6
- primaries: bfloat16 [192, 2, 8192, 256], P('freq', None, 'src'), may hold values from -0.0625 to 0.0625
- wavelet_ratio: float32 [2, 192], P(None, 'freq'), may hold values from -4 to 4
- window_lengths: int32 [16], replicated, may hold values from 1 to 32, 384 in all
- event_mask: int32 [512], P('freq'), may hold values 0 or 1
- pairing: int32 [16], replicated, may hold values from 0 to 15, each once
- old_traces: bfloat16 [512, 256, 256], P('freq', 'src'), may hold values from -6 to 6
- data_traces: bfloat16 [512, 256, 256], P('freq', 'src'), may hold values from -6 to 6
Outputs:
- new_traces: bfloat16 [512, 256, 256], P('freq', 'src')
The draws below stay inside these ranges and needn't reach their ends.
Inputs may be any that keep to these rules, and one draw needn't show every extreme that they name: `window_lengths`: each window holds 1 to 32 samples, the windows together hold 384, and one holds exactly 32. `pairing`: a permutation of the 16 blocks.
All inputs are finite; a program needn't handle non-finite values. No bound on the sum of `event_mask` on one device may be relied on, other than what follows from the above.
Results may differ from the reference program's by a relative error of at most 0.001.
Values sent between devices are 32-bit elements; how exact they have to be, the bound alone decides.
No kernel may reach another device: no remote copies, remote signals or barrier semaphores. Data moves between devices by JAX's collectives and lax.ppermute only.
A program may use at most 192 MiB of HBM per device.

```python
import math
import jax
import jax.numpy as jnp
import numpy as np
from jax import lax

K = 8192
F = 192
W = 256
NT = 384
TCAP = 32
TSLOTS = 512
N_FREQ = 16
N_SRC = 16


def place_ends(values, own_key, least, largest):
    index_at = [jax.random.randint(jax.random.fold_in(own_key, axis), (), 0, length) for axis, length in enumerate(values.shape)]
    main_axis = values.shape.index(max(values.shape))
    neighbour = index_at[:main_axis] + [(index_at[main_axis] + 1) % values.shape[main_axis]] + index_at[main_axis + 1:]
    return values.at[tuple(index_at)].set(least).at[tuple(neighbour)].set(largest)


def raised(array, rng, source, target, blocks, factor):
    owner, partner = [(jnp.arange(array.shape[position]) // (array.shape[position] // blocks)).reshape([-1 if axis == position else 1 for axis in range(array.ndim)]) for position in (source, target)]
    chosen = jax.random.permutation(rng, blocks)[partner]
    strong = (owner == chosen) | (owner == (partner + blocks // 2) % blocks)
    return jnp.where(strong, factor * array, array)


def block_scale(key, extent, split, smallest, largest):
    loudness = 1.0
    for axis_at, blocks in split:
        heights = jax.random.uniform(jax.random.fold_in(jax.random.fold_in(key, 6), axis_at), (blocks,), jnp.float32, smallest / len(split), largest / len(split))
        loudness = loudness * jnp.repeat(jnp.exp(heights), extent[axis_at] // blocks).reshape((-1,) + (1,) * (len(extent) - 1 - axis_at))
    return loudness


def length_profile(count, total, most, slope):
    portions = [(1 << 20) // math.isqrt(standing ** slope) + 1 for standing in range(2, count + 1)]
    spare, counts = total - most - (count - 1), [1] * (count - 1)
    while spare > 0:
        movable = [i for i in range(count - 1) if counts[i] < most]
        pool, budget = sum([portions[i] for i in movable]), spare
        for i in movable:
            addition = min(most - counts[i], max(1, budget * portions[i] // pool), spare)
            counts[i] = counts[i] + addition
            spare = spare - addition
    return np.array([most] + counts)


def uneven(own_key, amount, total, most, slope):
    if amount == 2:
        one = jax.random.randint(own_key, (), max(1, total - most), min(most, total - 1) + 1)
        return jnp.stack([one, total - one])
    lengths = jnp.asarray(length_profile(amount, total, most, slope), jnp.int32)
    twos = (amount - 1) // 2
    source_of, taker = lengths[1:1 + 2 * twos:2], lengths[2:2 + 2 * twos:2]
    room = jnp.minimum(source_of - 1, most - taker)
    passed = jax.random.randint(jax.random.fold_in(own_key, 1), (twos,), 0, 1 << 20) % (room + 1)
    lengths = lengths.at[1:1 + 2 * twos:2].set(source_of - passed).at[2:2 + 2 * twos:2].set(taker + passed)
    return lengths[jax.random.permutation(jax.random.fold_in(own_key, 2), amount)]


def gaussian(own_key, dims, scale, reach, shards=(), kind=jnp.bfloat16):
    entries = jax.random.normal(own_key, dims, jnp.float32) * scale
    if len(shards) > 0:
        entries = block_scale(own_key, dims, shards, -0.22, 0.18) * entries
    return jnp.clip(entries, min=-reach, max=reach).astype(kind)


def heavy_noise(key, shape, width, limit, pieces, heavy, held_as=jnp.bfloat16):
    array = width * jax.random.normal(key, shape, jnp.float32)
    if pieces:
        array = array * block_scale(key, shape, pieces, -0.22, 0.18)
    return jnp.clip(raised(array, jax.random.fold_in(key, 3), *heavy), -limit, limit).astype(held_as)


def setup_inputs(seed: int = 0) -> dict:
    streams_of = jax.random.split(jax.random.key(seed), 9)
    spectra = heavy_noise(streams_of[0], (F, 2, W, K), 1.0, 6.0, ((0, 16), (3, 16)), (3, 2, 16, 2.0))
    primaries = gaussian(streams_of[1], (F, 2, K, W), K ** -0.5, 0.0625, ((0, 16), (2, 16)))
    wavelet_ratio = gaussian(streams_of[2], (2, F), 1.0, 4.0, ((1, 16),), jnp.float32)
    window_lengths = uneven(streams_of[3], N_FREQ, NT, TCAP, 2).astype(jnp.int32)
    event_mask = place_ends((jax.random.randint(streams_of[4], (TSLOTS,), 0, 2) < 1).astype(jnp.int32), jax.random.fold_in(streams_of[4], 1), 0, 1)
    pairing = jax.random.permutation(streams_of[5], N_SRC).astype(jnp.int32)
    old_traces = gaussian(streams_of[6], (TSLOTS, W, W), 1.0, 6.0, ((0, 16), (1, 16)))
    data_traces = gaussian(streams_of[7], (TSLOTS, W, W), 1.0, 6.0, ((0, 16), (1, 16)))
    return {"spectra": spectra, "primaries": primaries, "wavelet_ratio": wavelet_ratio, "window_lengths": window_lengths, "event_mask": event_mask, "pairing": pairing, "old_traces": old_traces, "data_traces": data_traces}


shrink_level = 0.25
step_weight = 0.5

def time_basis(slots, freqs, window_lengths, capacity):
    starts = jnp.cumsum(window_lengths) - window_lengths
    window = slots // capacity
    offset = slots % capacity
    select = window[:, None] == jnp.arange(window_lengths.shape[0], dtype=jnp.int32)[None, :]
    begin = lax.optimization_barrier(jnp.sum(jnp.where(select, starts[None, :], 0), axis=1))
    length = lax.optimization_barrier(jnp.sum(jnp.where(select, window_lengths[None, :], 0), axis=1))
    inside = offset < length
    phase = (begin + offset)[:, None] * freqs[None, :] % NT
    angle = phase.astype(jnp.float32) * (2.0 * math.pi / NT)
    scale = jnp.where(inside, 1.0 / math.sqrt(F), 0.0).astype(jnp.float32)[:, None]
    basis = jnp.stack([jnp.cos(angle) * scale, -jnp.sin(angle) * scale], axis=2)
    return (basis, inside)

def reference(spectra, primaries, wavelet_ratio, window_lengths, event_mask, pairing, old_traces, data_traces):
    block_rows = W // N_SRC
    row_ids = jnp.arange(W, dtype=jnp.int32)
    inverse = jnp.zeros((N_SRC,), jnp.int32).at[pairing].set(jnp.arange(N_SRC, dtype=jnp.int32))
    mirror_cols = pairing[row_ids // block_rows] * block_rows + row_ids % block_rows
    mirror_rows = inverse[row_ids // block_rows] * block_rows + row_ids % block_rows

    def one_freq(freq):
        stacked_left = spectra[freq].reshape(2 * W, K)
        stacked_right = jnp.concatenate([primaries[freq, 0], primaries[freq, 1]], axis=1)
        product = jnp.dot(stacked_left, stacked_right, preferred_element_type=jnp.float32)
        real_part = product[:W, :W] - product[W:, W:]
        imag_part = product[:W, W:] + product[W:, :W]
        sym_real = 0.5 * (real_part + real_part[mirror_rows][:, mirror_cols].T)
        sym_imag = 0.5 * (imag_part + imag_part[mirror_rows][:, mirror_cols].T)
        ratio_real = wavelet_ratio[0, freq]
        ratio_imag = wavelet_ratio[1, freq]
        return jnp.stack([ratio_real * sym_real - ratio_imag * sym_imag, ratio_real * sym_imag + ratio_imag * sym_real])
    weighted = lax.map(one_freq, jnp.arange(F, dtype=jnp.int32))
    slots = jnp.arange(TSLOTS, dtype=jnp.int32)
    basis, inside = time_basis(slots, jnp.arange(F, dtype=jnp.int32), window_lengths, TCAP)
    traces = jnp.einsum('tfc,fcrs->trs', basis, weighted, precision=lax.Precision.HIGHEST)
    older = old_traces.astype(jnp.float32)
    events = event_mask.astype(jnp.float32)[:, None, None]
    moved = older + step_weight * events * (data_traces.astype(jnp.float32) - older - traces)
    shrunk = jnp.sign(moved) * jnp.maximum(jnp.abs(moved) - shrink_level, 0.0)
    return jnp.where(inside[:, None, None], shrunk, 0.0).astype(jnp.bfloat16)
```

```python
import functools
import math

import jax
import jax.numpy as jnp
from jax import lax
from jax.experimental import pallas as pl
from jax.experimental.pallas import tpu as pltpu
from jax.sharding import Mesh, PartitionSpec as P

F = 192
NT = 384
LANES = 128
BLOCK = 16
CHUNKS = (12,)

shrink_level = 0.25
step_weight = 0.5


def product_kernel(first, zi, ratio, spectra, primaries, relabel, out):
    step = pl.program_id(0)
    width = spectra.shape[2]
    depth = spectra.shape[3]
    rings = out.shape[0]
    half = width // 2
    parts = out.shape[1]
    groups = parts // 17
    rows = 8 * groups
    left = spectra[0].reshape(2 * width, depth)
    right = [
        jnp.dot(primaries[0, b], relabel[...], preferred_element_type=jnp.float32).astype(
            jnp.bfloat16
        )
        for b in range(2)
    ]
    by_real = jnp.dot(left, right[0], preferred_element_type=jnp.float32)
    by_imag = jnp.dot(left, right[1], preferred_element_type=jnp.float32)
    real = by_real[:width] - by_imag[width:]
    imag = by_imag[:width] + by_real[width:]
    real = 0.5 * (real + real.T)
    imag = 0.5 * (imag + imag.T)
    wr = ratio[0, first + step]
    wi = ratio[1, first + step]
    lane = lax.broadcasted_iota(jnp.int32, (BLOCK, LANES), 1)
    for c, z in enumerate((wr * real - wi * imag, wr * imag + wi * real)):
        row = 2 * step + c
        slot = row % 8
        for t in range(rings):
            k = lax.rem(t - zi[0] + rings, rings)
            low = z[BLOCK * t : BLOCK * (t + 1)]
            high = z[half + BLOCK * t : half + BLOCK * (t + 1)]
            if t:
                high = jnp.concatenate(
                    [high[:, half + BLOCK * t :], high[:, : BLOCK * t]], axis=1
                )
            else:
                high = high[:, half:]
            out[k, row] = low[:, BLOCK * t : BLOCK * t + LANES]
            out[k, rows + row] = high
            opposite = pltpu.roll(low[:, half:], lax.rem(BLOCK * (slot - t) + LANES, LANES), 1)
            place = 2 * rows + row // 8
            mine = (lane >= BLOCK * slot) & (lane < BLOCK * slot + BLOCK)
            out[k, place] = jnp.where(mine, opposite, out[k, place])


def product(spectra, primaries, ratio, relabel, zi, first, count):
    width, depth = spectra.shape[2:]
    parts = 17 * (2 * count // 8)
    return pl.pallas_call(
        functools.partial(product_kernel, first),
        grid=(count,),
        in_specs=[
            pl.BlockSpec(memory_space=pltpu.SMEM),
            pl.BlockSpec(memory_space=pltpu.SMEM),
            pl.BlockSpec((1, 2, width, depth), lambda i: (first + i, 0, 0, 0)),
            pl.BlockSpec((1, 2, depth, width), lambda i: (first + i, 0, 0, 0)),
            pl.BlockSpec((width, width), lambda i: (0, 0)),
        ],
        out_specs=pl.BlockSpec((8, parts, BLOCK, LANES), lambda i: (0, 0, 0, 0)),
        out_shape=jax.ShapeDtypeStruct((8, parts, BLOCK, LANES), jnp.float32),
        compiler_params=pltpu.CompilerParams(vmem_limit_bytes=40 * 1024 * 1024),
        cost_estimate=pl.CostEstimate(
            flops=count * 2 * 2 * width * 2 * width * depth,
            bytes_accessed=count * 8 * width * depth + 8 * parts * BLOCK * LANES * 4,
            transcendentals=0,
        ),
        name="product",
    )(zi, ratio, spectra, primaries, relabel)


def exchange_lanes(tiles):
    lane = lax.broadcasted_iota(jnp.int32, tiles[0].shape, 1) // BLOCK
    for bit in (1, 2, 4):
        upper = (lane // bit) % 2 == 1
        out = list(tiles)
        for a in range(8):
            if a & bit:
                continue
            x, y = tiles[a], tiles[a | bit]
            out[a] = jnp.where(upper, pltpu.roll(y, BLOCK * bit, 1), x)
            out[a | bit] = jnp.where(upper, y, pltpu.roll(x, LANES - BLOCK * bit, 1))
        tiles = out
    return tiles


def pack_kernel(place, own, up, down, keep, give, mail):
    yl, zi = place[0], place[1]
    groups = own.shape[0] // 17
    rows = 8 * groups
    lane = lax.broadcasted_iota(jnp.int32, (BLOCK, LANES), 1)

    def total(i):
        return own[i] + up[i] + down[i]

    for g in range(groups):
        for h in range(2):
            tiles = [total(rows * h + 8 * g + a) for a in range(8)]
            for a in range(8):

                @pl.when(yl == h)
                def _():
                    keep[8 * g + a] = tiles[a]

                @pl.when(yl != h)
                def _():
                    give[8 * g + a] = tiles[a]

            swapped = exchange_lanes(tiles)
            for m in range(1, 8):
                mail[lax.rem(zi + 8 * h + m, 16), g] = swapped[m]
        opposite = total(2 * rows + g)
        mail[zi + 8, g] = opposite
        flipped = jnp.zeros((BLOCK, LANES), jnp.float32)
        turned = opposite.T
        for a in range(8):
            block = jnp.concatenate(
                [turned[BLOCK * a : BLOCK * (a + 1)], jnp.zeros((BLOCK, LANES - BLOCK), jnp.float32)],
                axis=1,
            )
            flipped = flipped + (pltpu.roll(block, BLOCK * a, 1) if a else block)
        mail[zi, g] = flipped


def pack(place, own, up, down):
    groups = own.shape[0] // 17
    whole = pl.BlockSpec(memory_space=pltpu.VMEM)
    return pl.pallas_call(
        pack_kernel,
        in_specs=[pl.BlockSpec(memory_space=pltpu.SMEM), whole, whole, whole],
        out_specs=[whole, whole, whole],
        out_shape=[
            jax.ShapeDtypeStruct((8 * groups, BLOCK, LANES), jnp.float32),
            jax.ShapeDtypeStruct((8 * groups, BLOCK, LANES), jnp.float32),
            jax.ShapeDtypeStruct((16, groups, BLOCK, LANES), jnp.float32),
        ],
        name="pack",
    )(place, own, up, down)


def join_kernel(place, keep, got, mail, out):
    zi = place[1]
    groups = mail.shape[1]
    for g in range(groups):
        stack = []
        for k in range(8):
            z = lax.rem(zi + k, 8)
            stack.append(mail[z, g] + mail[z + 8, g])
        turned = jnp.concatenate(stack, axis=0).T.reshape(8, BLOCK, LANES)
        direct = keep[8 * g : 8 * g + 8] + got[8 * g : 8 * g + 8]
        out[:, 8 * g : 8 * g + 8, :LANES] = jnp.swapaxes(direct, 0, 1)
        out[:, 8 * g : 8 * g + 8, LANES:] = jnp.swapaxes(turned, 0, 1)


def join(place, keep, got, mail):
    groups = mail.shape[1]
    whole = pl.BlockSpec(memory_space=pltpu.VMEM)
    return pl.pallas_call(
        join_kernel,
        in_specs=[pl.BlockSpec(memory_space=pltpu.SMEM), whole, whole, whole],
        out_specs=whole,
        out_shape=jax.ShapeDtypeStruct((BLOCK, 8 * groups, 2 * LANES), jnp.float32),
        name="join",
    )(place, keep, got, mail)


def transform_kernel(basis, data, relabel, out):
    placed = jnp.dot(
        data[...],
        relabel[...],
        precision=lax.Precision.HIGHEST,
        preferred_element_type=jnp.float32,
    )
    out[...] = jnp.dot(
        basis[...], placed, precision=lax.Precision.HIGHEST, preferred_element_type=jnp.float32
    )


def transform(basis, data, relabel):
    whole = pl.BlockSpec(memory_space=pltpu.VMEM)
    return pl.pallas_call(
        transform_kernel,
        in_specs=[whole] * 3,
        out_specs=whole,
        out_shape=jax.ShapeDtypeStruct((basis.shape[0], data.shape[1]), jnp.float32),
        compiler_params=pltpu.CompilerParams(vmem_limit_bytes=40 * 1024 * 1024),
        name="transform",
    )(basis, data, relabel)


def update_kernel(events, inside, traces, older, data, out):
    count = older.shape[0]
    for t in range(count):
        old = older[t].astype(jnp.float32)
        moved = old + step_weight * events[t] * (
            data[t].astype(jnp.float32) - old - traces[:, t, :]
        )
        size = jnp.maximum(jnp.abs(moved) - shrink_level, 0.0)
        shrunk = jnp.where(moved < 0.0, -size, size)
        out[t] = jnp.where(inside[t] > 0, shrunk, 0.0).astype(jnp.bfloat16)


def update(events, inside, traces, older, data):
    whole = pl.BlockSpec(memory_space=pltpu.VMEM)
    scalars = pl.BlockSpec(memory_space=pltpu.SMEM)
    return pl.pallas_call(
        update_kernel,
        in_specs=[scalars, scalars, whole, whole, whole],
        out_specs=whole,
        out_shape=jax.ShapeDtypeStruct(older.shape, jnp.bfloat16),
        name="update",
    )(events, inside, traces, older, data)


def slot_windows(slots, window_lengths, capacity):
    starts = jnp.cumsum(window_lengths) - window_lengths
    window = slots // capacity
    offset = slots % capacity
    select = window[:, None] == jnp.arange(window_lengths.shape[0], dtype=jnp.int32)[None, :]
    begin = jnp.sum(jnp.where(select, starts[None, :], 0), axis=1)
    length = jnp.sum(jnp.where(select, window_lengths[None, :], 0), axis=1)
    return begin + offset, offset < length


def time_basis(times, inside, freqs):
    phase = times[:, None] * freqs[None, :] % NT
    angle = phase.astype(jnp.float32) * (2.0 * math.pi / NT)
    scale = jnp.where(inside, 1.0 / math.sqrt(F), 0.0).astype(jnp.float32)[:, None]
    odd = (jnp.arange(freqs.shape[0]) % 2 == 1)[None, :]
    return jnp.where(odd, -jnp.sin(angle), jnp.cos(angle)) * scale


def ring(n, d):
    return [(i, (i + d) % n) for i in range(n)]


def add_head(base, head):
    n = head.shape[0]
    return jnp.concatenate([base[:n] + head, base[n:]])


def add_tail(base, tail):
    n = base.shape[0] - tail.shape[0]
    return jnp.concatenate([base[:n], base[n:] + tail])


def ring_sum(parts):
    up = functools.partial(lax.ppermute, axis_name="z", perm=ring(8, 1))
    down = functools.partial(lax.ppermute, axis_name="z", perm=ring(8, -1))
    cut = parts.shape[1] // 2
    a, b = up(parts[4, :cut]), down(parts[4, cut:])
    a, b = up(add_head(parts[3], a)), down(add_tail(parts[5], b))
    a, b = up(parts[2] + a), down(parts[6] + b)
    return parts[0], up(parts[1] + a), down(parts[7] + b)


def on_device(
    spectra, primaries, wavelet_ratio, window_lengths, event_mask, pairing, old_traces, data_traces
):
    src = ("yl", "z")
    freq = ("x", "yh", "core")
    freq_count = lax.axis_size(freq)
    freq_dev = spectra.shape[0]
    width = spectra.shape[2]
    capacity = old_traces.shape[0]
    yl, zi = lax.axis_index("yl"), lax.axis_index("z")
    own = yl * 8 + zi
    place = jnp.stack([yl, zi])
    lanes = jnp.arange(width, dtype=jnp.int32)
    blocks = lanes // BLOCK
    ids = jnp.arange(pairing.shape[0], dtype=jnp.int32)

    def paired(block):
        return jnp.sum(jnp.where(block[:, None] == ids[None, :], pairing[None, :], 0), axis=1)

    source = paired(blocks) * BLOCK + lanes % BLOCK
    relabel = (lanes[:, None] == source[None, :]).astype(jnp.bfloat16)
    target = paired((blocks + own) % pairing.shape[0]) * BLOCK + lanes % BLOCK
    restore = (target[:, None] == lanes[None, :]).astype(jnp.float32)
    slots = jnp.arange(capacity * freq_count, dtype=jnp.int32)
    times, inside = slot_windows(slots, window_lengths, capacity)
    basis = time_basis(
        times, inside, jnp.arange(2 * freq_dev * freq_count, dtype=jnp.int32) // 2
    )
    own_slots = lax.axis_index(freq) * capacity + jnp.arange(capacity, dtype=jnp.int32)
    _, inside_own = slot_windows(own_slots, window_lengths, capacity)

    first = 0
    joined = []
    for count in CHUNKS:
        parts = product(
            spectra, primaries, wavelet_ratio, relabel, zi.reshape(1), first, count
        )
        first += count
        keep, give, mail = pack(place, *ring_sum(parts))
        got = lax.ppermute(give, "yl", ring(2, 1))
        mail = lax.all_to_all(mail, src, split_axis=0, concat_axis=0, tiled=True)
        joined.append(join(place, keep, got, mail))
    whole = joined[0] if len(joined) == 1 else jnp.concatenate(joined, axis=1)
    spread = lax.all_to_all(whole, freq, split_axis=0, concat_axis=0, tiled=True)
    slotted = transform(basis, spread.reshape(-1, width), restore)
    slotted = slotted.reshape(freq_count, capacity, width)
    traces = lax.all_to_all(slotted, freq, split_axis=0, concat_axis=0, tiled=True)
    return update(
        event_mask.astype(jnp.float32),
        inside_own.astype(jnp.int32),
        traces,
        old_traces,
        data_traces,
    )


def solution(mesh):
    shape = tuple(mesh.shape.values())
    cores = 2 if shape[0] % 2 == 0 else 1
    yh = 2 if shape[0] % 4 == 0 else 1
    devices = mesh.devices.reshape(shape[0] // (cores * yh), yh, cores, shape[1] // 8, 8)
    split = Mesh(devices, ("x", "yh", "core", "yl", "z"))
    freq = ("x", "yh", "core")
    src = ("yl", "z")
    in_specs = (
        P(freq, None, None, src),
        P(freq, None, src, None),
        P(None, freq),
        P(),
        P(freq),
        P(),
        P(freq, src, None),
        P(freq, src, None),
    )
    return jax.shard_map(
        on_device, mesh=split, in_specs=in_specs, out_specs=P(freq, src, None), check_vma=False
    )
```

```python
import functools
import math

import jax
import jax.numpy as jnp
from jax import lax
from jax.experimental import pallas as pl
from jax.experimental.pallas import tpu as pltpu
from jax.sharding import Mesh, PartitionSpec as P

F = 192
NT = 384
LANES = 128
BLOCK = 16
RING = 8
PRODUCT_VMEM = 59 * 1024 * 1024
SMALL_VMEM = 24 * 1024 * 1024

shrink_level = 0.25
step_weight = 0.5


def window(near, far, shift):
    lane = lax.broadcasted_iota(jnp.int32, near.shape, 1)
    row = lax.broadcasted_iota(jnp.int32, near.shape, 0)
    if shift:
        near = pltpu.roll(near, LANES - shift, 1)
        far = pltpu.roll(far, LANES - shift, 1)
    return jnp.where((lane < LANES - shift) & (lane >= row), near, far)


def product_kernel(
    pairing, ratio, spectra, primaries, keep_first, keep, give_first, give, own,
    left, right, relabel, relabel_low, chosen, held, out, slots, left_sems, right_sems, out_sems,
):
    freqs, _, width, depth = left.shape
    count = freqs // 2
    half = width // 2
    rows = 2 * count
    tail = 2 * rows * BLOCK
    core, zi = lax.axis_index("core"), lax.axis_index("z")
    lane = lax.broadcasted_iota(jnp.int32, (BLOCK, LANES), 1)
    level = lax.broadcasted_iota(jnp.int32, (BLOCK, LANES), 0)

    def fetch_left(i):
        return pltpu.make_async_copy(spectra.at[i], left.at[i], left_sems.at[i])

    def fetch_right(i):
        return pltpu.make_async_copy(primaries.at[i], right.at[i], right_sems.at[i])

    for i in range(freqs):
        fetch_right(i).start()
        fetch_left(i).start()
    block = lax.broadcasted_iota(jnp.int32, (8, width), 1) // BLOCK
    source = jnp.zeros((8, width), jnp.int32)
    for b in range(width // BLOCK):
        source = jnp.where(block == b, pairing[b], source)
    source = source * BLOCK + lax.broadcasted_iota(jnp.int32, (8, width), 1) % BLOCK
    for r in range(0, width, 8):
        row = lax.broadcasted_iota(jnp.int32, (8, width), 0) + r
        relabel[r : r + 8] = jnp.where(row == source, 1.0, 0.0)
    relabel_low[...] = relabel[...].astype(jnp.bfloat16)
    out[:, tail:] = jnp.zeros((out.shape[0], out.shape[1] - tail, LANES), out.dtype)
    for second in range(2):
        long_up = second == core
        for t in range(RING):
            k = lax.rem(t - zi + RING, RING)
            away = jnp.where(k <= 4, 4 - k, k - 4)
            goes_up = (k < 4) | ((k == 4) & long_up)
            send = 2 * away - jnp.where(long_up == goes_up, 0, 1)
            mine = goes_up == (core == 0)
            slots[second, t] = jnp.where(k == 0, 14 + second, send + jnp.where(mine, 0, 7))

    def cut(i):
        second = lax.div(i, count)
        real, imag = held[i & 1, 0], held[i & 1, 1]
        real = 0.5 * (real + real.T)
        imag = 0.5 * (imag + imag.T)
        wr = ratio[0, i]
        wi = ratio[1, i]
        for c, z in enumerate((wr * real - wi * imag, wr * imag + wi * real)):
            row = 2 * i + c
            shift = row & 7
            place = tail + (row >> 3) - second * (2 * count // 8)
            row = row - second * rows
            for t in range(RING):
                k = slots[second, t]
                low = z[BLOCK * t : BLOCK * (t + 1)]
                high = z[half + BLOCK * t : half + BLOCK * (t + 1)]
                out[k, pl.ds(pl.multiple_of(row * BLOCK, BLOCK), BLOCK)] = window(
                    low[:, :half], low[:, half:], BLOCK * t
                )
                out[k, pl.ds(pl.multiple_of((rows + row) * BLOCK, BLOCK), BLOCK)] = window(
                    high[:, half:], high[:, :half], BLOCK * t
                )
                middle = jnp.where(lane == level + BLOCK * t, low[:, half:], 0.0)
                middle = jnp.sum(middle, axis=0, keepdims=True)
                middle = pltpu.roll(middle, (BLOCK * (shift - t)) & (LANES - 1), 1)
                out[k, pl.ds(place, 1)] += middle

    def multiply(i):
        a = left[i].reshape(2 * width, depth)
        by_real = jnp.dot(a, chosen[i & 1, 0], preferred_element_type=jnp.float32)
        by_imag = jnp.dot(a, chosen[i & 1, 1], preferred_element_type=jnp.float32)
        held[i & 1, 0] = by_real[:width] - by_imag[width:]
        held[i & 1, 1] = by_imag[:width] + by_real[width:]

    def choose(i):
        for b in range(2):
            chosen[i & 1, b] = jnp.dot(
                right[i, b], relabel_low[...], preferred_element_type=jnp.float32
            ).astype(jnp.bfloat16)

    def stages(i, carry):
        fetch_right(i).wait()
        fetch_left(i - 1).wait()
        cut(i - 2)
        multiply(i - 1)
        choose(i)
        return carry

    def copies(moves):
        return [
            pltpu.make_async_copy(out.at[slot], dst.at[i], out_sems.at[slot])
            for slot, dst, i in moves
        ]

    early = copies(
        [(0, keep_first, 0)]
        + [(n, keep, n - 1) for n in (2, 4, 6)]
        + [(7 + n, give, n - 1) for n in (1, 3, 5)]
        + [(14, own, 0)]
    )
    late = copies(
        [(7, give_first, 0)]
        + [(n, keep, n - 1) for n in (1, 3, 5)]
        + [(7 + n, give, n - 1) for n in (2, 4, 6)]
        + [(15, own, 1)]
    )
    fetch_right(0).wait()
    choose(0)
    fetch_right(1).wait()
    fetch_left(0).wait()
    multiply(0)
    choose(1)
    lax.fori_loop(2, count + 2, stages, 0)
    for copy in early:
        copy.start()
    lax.fori_loop(count + 2, freqs, stages, 0)
    fetch_left(freqs - 1).wait()
    cut(freqs - 2)
    multiply(freqs - 1)
    cut(freqs - 1)
    for copy in late:
        copy.start()
    for copy in early + late:
        copy.wait()


def product(spectra, primaries, ratio, pairing):
    freqs = spectra.shape[0]
    width, depth = spectra.shape[2:]
    height = 2 * freqs * BLOCK + 8
    smem = pl.BlockSpec(memory_space=pltpu.SMEM)
    anywhere = pl.BlockSpec(memory_space=pl.ANY)
    shapes = [(n, height, LANES) for n in (1, 6, 1, 6, 2)]
    return pl.pallas_call(
        product_kernel,
        in_specs=[smem, smem, anywhere, anywhere],
        out_specs=[anywhere] * 5,
        out_shape=[jax.ShapeDtypeStruct(s, jnp.float32) for s in shapes],
        scratch_shapes=[
            pltpu.VMEM(spectra.shape, spectra.dtype),
            pltpu.VMEM(primaries.shape, primaries.dtype),
            pltpu.VMEM((width, width), jnp.float32),
            pltpu.VMEM((width, width), jnp.bfloat16),
            pltpu.VMEM((2, 2, depth, width), jnp.bfloat16),
            pltpu.VMEM((2, 2, width, width), jnp.float32),
            pltpu.VMEM((16, height, LANES), jnp.float32),
            pltpu.SMEM((2, RING), jnp.int32),
            pltpu.SemaphoreType.DMA((freqs,)),
            pltpu.SemaphoreType.DMA((freqs,)),
            pltpu.SemaphoreType.DMA((16,)),
        ],
        compiler_params=pltpu.CompilerParams(vmem_limit_bytes=PRODUCT_VMEM),
        cost_estimate=pl.CostEstimate(
            flops=freqs * 2 * 2 * width * 2 * width * depth,
            bytes_accessed=freqs * 8 * width * depth + 16 * height * LANES * 4,
            transcendentals=0,
        ),
        name="product",
    )(pairing, ratio, spectra, primaries)


def collect_kernel(keep, got, *refs):
    arrived, out = refs[:-2], refs[-1]
    for i, part in enumerate((keep, got)):
        out[i] = arrived[0][i] + part[0] if arrived else part[0]


def collect(index, keep, got, before, *arrived):
    shape = (2,) + keep.shape[1:]
    one = pl.BlockSpec((1,) + shape[1:], lambda i: (index, 0, 0))
    whole = pl.BlockSpec(shape, lambda i: (0, 0, 0))
    return pl.pallas_call(
        collect_kernel,
        grid=(1,),
        in_specs=[one, one] + [whole] * len(arrived) + [pl.BlockSpec(memory_space=pl.ANY)],
        out_specs=whole,
        out_shape=jax.ShapeDtypeStruct(shape, jnp.float32),
        compiler_params=pltpu.CompilerParams(vmem_limit_bytes=SMALL_VMEM),
        name="collect",
    )(keep, got, *arrived, before)


def exchange_lanes(tiles):
    lane = lax.broadcasted_iota(jnp.int32, tiles[0].shape, 1) // BLOCK
    for bit in (1, 2, 4):
        upper = (lane // bit) % 2 == 1
        out = list(tiles)
        for a in range(8):
            if a & bit:
                continue
            x, y = tiles[a], tiles[a | bit]
            out[a] = jnp.where(upper, pltpu.roll(y, BLOCK * bit, 1), x)
            out[a | bit] = jnp.where(upper, y, pltpu.roll(x, LANES - BLOCK * bit, 1))
        tiles = out
    return tiles


def ring_total(refs, half, start, size=BLOCK):
    own, late, early, got_late, got_early = refs
    at = pl.ds(start, size)
    if half:
        return own[1, at] + early[0, at] + got_late[at]
    return own[0, at] + late[0, at] + got_early[at]


def direct_kernel(*refs):
    keep, give = refs[5:]
    yl = lax.axis_index("yl")
    rows = keep.shape[0] // 2
    for half in range(2):
        for a in range(rows):
            for h, dst in ((yl, keep), (1 - yl, give)):
                start = pl.multiple_of(BLOCK * (rows * h + a), BLOCK)
                dst[rows * half + a] = ring_total(refs[:5], half, start)


def turn_blocks(x):
    turned = x.T
    out = jnp.zeros(x.shape, x.dtype)
    for a in range(8):
        block = jnp.concatenate(
            [turned[BLOCK * a : BLOCK * (a + 1)], jnp.zeros((BLOCK, LANES - BLOCK), x.dtype)],
            axis=1,
        )
        out = out + (pltpu.roll(block, BLOCK * a, 1) if a else block)
    return out


def mail_kernel(*refs):
    mail = refs[5]
    zi = lax.axis_index("z")
    groups = mail.shape[1]
    rows = 4 * groups
    across = lax.broadcasted_iota(jnp.int32, (BLOCK, LANES), 1) % BLOCK
    down = lax.broadcasted_iota(jnp.int32, (BLOCK, LANES), 0)

    for g in range(groups):
        firsts = []
        for h in range(2):
            tiles = [
                ring_total(refs[:5], row // rows, BLOCK * (rows * h + row % rows))
                for row in range(8 * g, 8 * g + 8)
            ]
            swapped = exchange_lanes(tiles)
            firsts.append(swapped[0])
            for m in range(1, 8):
                mail[lax.rem(zi + 8 * h + m, 16), g] = swapped[m]
        middle = 0.0
        for half in range(2):
            if rows * half < 8 * g + 8 and rows * (half + 1) > 8 * g:
                place = 2 * rows * BLOCK + g - rows * half // 8
                middle = middle + ring_total(refs[:5], half, place, 1)
        for at, below, above in ((8, firsts[0], firsts[1]), (0, firsts[1], firsts[0])):
            mail[zi + at, g] = jnp.where(
                across < down, below, jnp.where(across == down, middle, turn_blocks(above))
            )


def pack(rows, *sums):
    whole = pl.BlockSpec(memory_space=pltpu.VMEM)

    def call(kernel, shapes, name):
        return pl.pallas_call(
            kernel,
            in_specs=[whole] * 5,
            out_specs=[whole] * len(shapes),
            out_shape=[jax.ShapeDtypeStruct(s, jnp.float32) for s in shapes],
            compiler_params=pltpu.CompilerParams(vmem_limit_bytes=SMALL_VMEM),
            name=name,
        )(*sums)

    keep, give = call(direct_kernel, [(rows, BLOCK, LANES)] * 2, "direct")
    (mail,) = call(mail_kernel, [(16, rows // 8, BLOCK, LANES)], "mail")
    return keep, give, mail


def join_kernel(keep, got, mail, out):
    zi = lax.axis_index("z")
    groups = mail.shape[1]
    lane = lax.broadcasted_iota(jnp.int32, (BLOCK, LANES), 1)
    level = lax.broadcasted_iota(jnp.int32, (BLOCK, LANES), 0)
    rest = jnp.zeros((BLOCK, LANES - BLOCK), jnp.float32)
    for g in range(groups):
        stack = []
        for k in range(8):
            z = lax.rem(zi + k, 8)
            stack.append(mail[z, g] + mail[z + 8, g])
        turned = jnp.concatenate(stack, axis=0).T.reshape(8, BLOCK, LANES)
        tiles = [keep[8 * g + a] + got[8 * g + a] for a in range(8)]
        packed = jnp.where(lane < BLOCK, tiles[0], 0.0)
        for a in range(1, 8):
            packed = packed + pltpu.roll(jnp.where(lane < BLOCK, tiles[a], 0.0), BLOCK * a, 1)
        upper = packed.T
        direct = jnp.stack(
            [
                jnp.where(
                    lane < level,
                    jnp.concatenate([upper[BLOCK * a : BLOCK * (a + 1)], rest], axis=1),
                    tiles[a],
                )
                for a in range(8)
            ]
        )
        out[:, 8 * g : 8 * g + 8, :LANES] = jnp.swapaxes(direct, 0, 1)
        out[:, 8 * g : 8 * g + 8, LANES:] = jnp.swapaxes(turned, 0, 1)


def join(keep, got, mail):
    groups = mail.shape[1]
    whole = pl.BlockSpec(memory_space=pltpu.VMEM)
    return pl.pallas_call(
        join_kernel,
        in_specs=[whole] * 3,
        out_specs=whole,
        out_shape=jax.ShapeDtypeStruct((BLOCK, 8 * groups, 2 * LANES), jnp.float32),
        compiler_params=pltpu.CompilerParams(vmem_limit_bytes=SMALL_VMEM),
        name="join",
    )(keep, got, mail)


def transform_kernel(basis, data, relabel, out):
    dot = functools.partial(jnp.dot, preferred_element_type=jnp.float32)
    x = data[...]
    high = x.astype(jnp.bfloat16)
    low = (x - high.astype(jnp.float32)).astype(jnp.bfloat16)
    high = dot(high, relabel[...]).astype(jnp.bfloat16)
    low = dot(low, relabel[...]).astype(jnp.bfloat16)
    out[...] = dot(basis[0], high) + (dot(basis[0], low) + dot(basis[1], high))


def transform(basis, data, relabel):
    whole = pl.BlockSpec(memory_space=pltpu.VMEM)
    return pl.pallas_call(
        transform_kernel,
        in_specs=[whole] * 3,
        out_specs=whole,
        out_shape=jax.ShapeDtypeStruct((basis.shape[1], data.shape[1]), jnp.float32),
        compiler_params=pltpu.CompilerParams(vmem_limit_bytes=SMALL_VMEM),
        name="transform",
    )(basis, data, relabel)


def update_kernel(events, inside, traces, older, data, out):
    count = older.shape[0]
    for t in range(count):
        old = older[t].astype(jnp.float32)
        moved = old + step_weight * events[t] * (
            data[t].astype(jnp.float32) - old - traces[:, t, :]
        )
        size = jnp.maximum(jnp.abs(moved) - shrink_level, 0.0)
        shrunk = jnp.where(moved < 0.0, -size, size)
        out[t] = jnp.where(inside[t] > 0, shrunk, 0.0).astype(jnp.bfloat16)


def update(events, inside, traces, older, data):
    whole = pl.BlockSpec(memory_space=pltpu.VMEM)
    scalars = pl.BlockSpec(memory_space=pltpu.SMEM)
    return pl.pallas_call(
        update_kernel,
        in_specs=[scalars, scalars, whole, whole, whole],
        out_specs=whole,
        out_shape=jax.ShapeDtypeStruct(older.shape, jnp.bfloat16),
        compiler_params=pltpu.CompilerParams(vmem_limit_bytes=SMALL_VMEM),
        name="update",
    )(events, inside, traces, older, data)


def slot_windows(slots, window_lengths, capacity):
    starts = jnp.cumsum(window_lengths) - window_lengths
    window = slots // capacity
    offset = slots % capacity
    select = window[:, None] == jnp.arange(window_lengths.shape[0], dtype=jnp.int32)[None, :]
    begin = jnp.sum(jnp.where(select, starts[None, :], 0), axis=1)
    length = jnp.sum(jnp.where(select, window_lengths[None, :], 0), axis=1)
    return begin + offset, offset < length


def time_basis(times, inside, freqs):
    phase = times[:, None] * freqs[None, :] % NT
    angle = phase.astype(jnp.float32) * (2.0 * math.pi / NT)
    scale = jnp.where(inside, 1.0 / math.sqrt(F), 0.0).astype(jnp.float32)[:, None]
    odd = (jnp.arange(freqs.shape[0]) % 2 == 1)[None, :]
    return jnp.where(odd, -jnp.sin(angle), jnp.cos(angle)) * scale


def ring(n, d):
    return [(i, (i + d) % n) for i in range(n)]


def other_half_kernel(arrived, before, out):
    out[...] = arrived[1]


def other_half(arrived, before):
    whole = pl.BlockSpec(memory_space=pltpu.VMEM)
    return pl.pallas_call(
        other_half_kernel,
        in_specs=[whole, pl.BlockSpec(memory_space=pl.ANY)],
        out_specs=whole,
        out_shape=jax.ShapeDtypeStruct(arrived.shape[1:], arrived.dtype),
        compiler_params=pltpu.CompilerParams(vmem_limit_bytes=SMALL_VMEM),
        name="other_half",
    )(arrived, before)


def ring_sums(keep_first, keep, give_first, give):
    swap = functools.partial(lax.ppermute, axis_name="core", perm=ring(2, 1))
    step = functools.partial(
        lax.ppermute,
        axis_name=("core", "z"),
        perm=[
            (c * RING + z, c * RING + (z + (1 if c == 0 else -1)) % RING)
            for c in range(2)
            for z in range(RING)
        ],
    )
    payload = collect(0, keep_first, swap(give_first), keep_first)
    payload, give = lax.optimization_barrier((payload, give))
    got = swap(give)
    flying = [step(payload)]
    for n in range(6):
        payload = collect(n, keep, got, payload, *flying[:-1])
        flying = flying[-1:] + [step(payload)]
    early, late = flying
    return late, early, swap(late[1]), swap(other_half(early, payload))


def on_device(
    spectra, primaries, wavelet_ratio, window_lengths, event_mask, pairing, old_traces, data_traces
):
    src = ("yl", "z")
    freq = ("x", "yh", "core")
    freq_count = lax.axis_size(freq)
    freq_dev = spectra.shape[0]
    width = spectra.shape[2]
    capacity = old_traces.shape[0]
    yl, zi = lax.axis_index("yl"), lax.axis_index("z")
    own = yl * 8 + zi
    lanes = jnp.arange(width, dtype=jnp.int32)
    blocks = lanes // BLOCK
    ids = jnp.arange(pairing.shape[0], dtype=jnp.int32)

    def paired(block):
        return jnp.sum(jnp.where(block[:, None] == ids[None, :], pairing[None, :], 0), axis=1)

    target = paired((blocks + own) % pairing.shape[0]) * BLOCK + lanes % BLOCK
    restore = (target[:, None] == lanes[None, :]).astype(jnp.bfloat16)
    slots = jnp.arange(capacity * freq_count, dtype=jnp.int32)
    times, inside = slot_windows(slots, window_lengths, capacity)
    basis = time_basis(
        times, inside, jnp.arange(2 * freq_dev * freq_count, dtype=jnp.int32) // 2
    )
    coarse = lax.reduce_precision(basis, 8, 7)
    basis = jnp.stack([coarse, basis - coarse]).astype(jnp.bfloat16)
    own_slots = lax.axis_index(freq) * capacity + jnp.arange(capacity, dtype=jnp.int32)
    _, inside_own = slot_windows(own_slots, window_lengths, capacity)

    *sends, ends = product(spectra, primaries, wavelet_ratio, pairing)
    keep, give, mail = pack(2 * freq_dev, ends, *ring_sums(*sends))
    got = lax.ppermute(give, "yl", ring(2, 1))
    mail = lax.all_to_all(mail, src, split_axis=0, concat_axis=0, tiled=True)
    whole = join(keep, got, mail)
    spread = lax.all_to_all(whole, freq, split_axis=0, concat_axis=0, tiled=True)
    slotted = transform(basis, spread.reshape(-1, width), restore)
    slotted = slotted.reshape(freq_count, capacity, width)
    traces = lax.all_to_all(slotted, freq, split_axis=0, concat_axis=0, tiled=True)
    return update(
        event_mask.astype(jnp.float32),
        inside_own.astype(jnp.int32),
        traces,
        old_traces,
        data_traces,
    )


def solution(mesh):
    shape = tuple(mesh.shape.values())
    cores = 2 if shape[0] % 2 == 0 else 1
    yh = 2 if shape[0] % 4 == 0 else 1
    devices = mesh.devices.reshape(shape[0] // (cores * yh), yh, cores, shape[1] // 8, 8)
    split = Mesh(devices, ("x", "yh", "core", "yl", "z"))
    freq = ("x", "yh", "core")
    src = ("yl", "z")
    in_specs = (
        P(freq, None, None, src),
        P(freq, None, src, None),
        P(None, freq),
        P(),
        P(freq),
        P(),
        P(freq, src, None),
        P(freq, src, None),
    )
    return jax.shard_map(
        on_device, mesh=split, in_specs=in_specs, out_specs=P(freq, src, None), check_vma=False
    )
```

```python
import functools
import math

import jax
import jax.numpy as jnp
from jax import lax
from jax.experimental import pallas as pl
from jax.experimental.pallas import tpu as pltpu
from jax.sharding import Mesh, PartitionSpec as P

F = 192
NT = 384
LANES = 128
BLOCK = 16
RING = 8
PRODUCT_VMEM = 59 * 1024 * 1024
SMALL_VMEM = 24 * 1024 * 1024

shrink_level = 0.25
step_weight = 0.5


def window(near, far, shift):
    lane = lax.broadcasted_iota(jnp.int32, near.shape, 1)
    row = lax.broadcasted_iota(jnp.int32, near.shape, 0)
    if shift:
        near = pltpu.roll(near, LANES - shift, 1)
        far = pltpu.roll(far, LANES - shift, 1)
    return jnp.where((lane < LANES - shift) & (lane >= row), near, far)


def product_kernel(
    pairing, ratio, spectra, primaries, keep_first, keep, give_first, give, own,
    left, right, relabel, relabel_low, chosen, held, out, slots, left_sems, right_sems, out_sems,
):
    freqs, _, width, depth = left.shape
    count = freqs // 2
    half = width // 2
    rows = 2 * count
    tail = 2 * rows * BLOCK
    core, zi = lax.axis_index("core"), lax.axis_index("z")
    lane = lax.broadcasted_iota(jnp.int32, (BLOCK, LANES), 1)
    level = lax.broadcasted_iota(jnp.int32, (BLOCK, LANES), 0)

    def fetch_left(i):
        return pltpu.make_async_copy(spectra.at[i], left.at[i], left_sems.at[i])

    def fetch_right(i):
        return pltpu.make_async_copy(primaries.at[i], right.at[i], right_sems.at[i])

    for i in range(freqs):
        fetch_right(i).start()
        fetch_left(i).start()
    block = lax.broadcasted_iota(jnp.int32, (8, width), 1) // BLOCK
    source = jnp.zeros((8, width), jnp.int32)
    for b in range(width // BLOCK):
        source = jnp.where(block == b, pairing[b], source)
    source = source * BLOCK + lax.broadcasted_iota(jnp.int32, (8, width), 1) % BLOCK
    for r in range(0, width, 8):
        row = lax.broadcasted_iota(jnp.int32, (8, width), 0) + r
        relabel[r : r + 8] = jnp.where(row == source, 1.0, 0.0)
    relabel_low[...] = relabel[...].astype(jnp.bfloat16)
    out[:, tail:] = jnp.zeros((out.shape[0], out.shape[1] - tail, LANES), out.dtype)
    for second in range(2):
        long_up = second == core
        for t in range(RING):
            k = lax.rem(t - zi + RING, RING)
            away = jnp.where(k <= 4, 4 - k, k - 4)
            goes_up = (k < 4) | ((k == 4) & long_up)
            send = 2 * away - jnp.where(long_up == goes_up, 0, 1)
            mine = goes_up == (core == 0)
            slots[second, t] = jnp.where(k == 0, 14 + second, send + jnp.where(mine, 0, 7))

    def cut(i):
        second = lax.div(i, count)
        real, imag = held[i & 1, 0], held[i & 1, 1]
        real = 0.5 * (real + real.T)
        imag = 0.5 * (imag + imag.T)
        wr = ratio[0, i]
        wi = ratio[1, i]
        for c, z in enumerate((wr * real - wi * imag, wr * imag + wi * real)):
            row = 2 * i + c
            shift = row & 7
            place = tail + (row >> 3) - second * (2 * count // 8)
            row = row - second * rows
            for t in range(RING):
                k = slots[second, t]
                low = z[BLOCK * t : BLOCK * (t + 1)]
                high = z[half + BLOCK * t : half + BLOCK * (t + 1)]
                out[k, pl.ds(pl.multiple_of(row * BLOCK, BLOCK), BLOCK)] = window(
                    low[:, :half], low[:, half:], BLOCK * t
                )
                out[k, pl.ds(pl.multiple_of((rows + row) * BLOCK, BLOCK), BLOCK)] = window(
                    high[:, half:], high[:, :half], BLOCK * t
                )
                middle = jnp.where(lane == level + BLOCK * t, low[:, half:], 0.0)
                middle = jnp.sum(middle, axis=0, keepdims=True)
                middle = pltpu.roll(middle, (BLOCK * (shift - t)) & (LANES - 1), 1)
                out[k, pl.ds(place, 1)] += middle

    def multiply(i):
        a = left[i].reshape(2 * width, depth)
        by_real = jnp.dot(a, chosen[i & 1, 0], preferred_element_type=jnp.float32)
        by_imag = jnp.dot(a, chosen[i & 1, 1], preferred_element_type=jnp.float32)
        held[i & 1, 0] = by_real[:width] - by_imag[width:]
        held[i & 1, 1] = by_imag[:width] + by_real[width:]

    def choose(i):
        for b in range(2):
            chosen[i & 1, b] = jnp.dot(
                right[i, b], relabel_low[...], preferred_element_type=jnp.float32
            ).astype(jnp.bfloat16)

    def stages(i, carry):
        fetch_right(i).wait()
        fetch_left(i - 1).wait()
        cut(i - 2)
        multiply(i - 1)
        choose(i)
        return carry

    def copies(moves):
        return [
            pltpu.make_async_copy(out.at[slot], dst.at[i], out_sems.at[slot])
            for slot, dst, i in moves
        ]

    early = copies(
        [(0, keep_first, 0)]
        + [(n, keep, n - 1) for n in (2, 4, 6)]
        + [(7 + n, give, n - 1) for n in (1, 3, 5)]
        + [(14, own, 0)]
    )
    late = copies(
        [(7, give_first, 0)]
        + [(n, keep, n - 1) for n in (1, 3, 5)]
        + [(7 + n, give, n - 1) for n in (2, 4, 6)]
        + [(15, own, 1)]
    )
    fetch_right(0).wait()
    choose(0)
    fetch_right(1).wait()
    fetch_left(0).wait()
    multiply(0)
    choose(1)
    lax.fori_loop(2, count + 2, stages, 0)
    for copy in early:
        copy.start()
    lax.fori_loop(count + 2, freqs, stages, 0)
    fetch_left(freqs - 1).wait()
    cut(freqs - 2)
    multiply(freqs - 1)
    cut(freqs - 1)
    for copy in late:
        copy.start()
    for copy in early + late:
        copy.wait()


def product(spectra, primaries, ratio, pairing):
    freqs = spectra.shape[0]
    width, depth = spectra.shape[2:]
    height = 2 * freqs * BLOCK + 8
    smem = pl.BlockSpec(memory_space=pltpu.SMEM)
    anywhere = pl.BlockSpec(memory_space=pl.ANY)
    shapes = [(n, height, LANES) for n in (1, 6, 1, 6, 2)]
    return pl.pallas_call(
        product_kernel,
        in_specs=[smem, smem, anywhere, anywhere],
        out_specs=[anywhere] * 5,
        out_shape=[jax.ShapeDtypeStruct(s, jnp.float32) for s in shapes],
        scratch_shapes=[
            pltpu.VMEM(spectra.shape, spectra.dtype),
            pltpu.VMEM(primaries.shape, primaries.dtype),
            pltpu.VMEM((width, width), jnp.float32),
            pltpu.VMEM((width, width), jnp.bfloat16),
            pltpu.VMEM((2, 2, depth, width), jnp.bfloat16),
            pltpu.VMEM((2, 2, width, width), jnp.float32),
            pltpu.VMEM((16, height, LANES), jnp.float32),
            pltpu.SMEM((2, RING), jnp.int32),
            pltpu.SemaphoreType.DMA((freqs,)),
            pltpu.SemaphoreType.DMA((freqs,)),
            pltpu.SemaphoreType.DMA((16,)),
        ],
        compiler_params=pltpu.CompilerParams(vmem_limit_bytes=PRODUCT_VMEM),
        cost_estimate=pl.CostEstimate(
            flops=freqs * 2 * 2 * width * 2 * width * depth,
            bytes_accessed=freqs * 8 * width * depth + 16 * height * LANES * 4,
            transcendentals=0,
        ),
        name="product",
    )(pairing, ratio, spectra, primaries)


def collect_kernel(keep, got, *refs):
    arrived, out = refs[:-2], refs[-1]
    for i, part in enumerate((keep, got)):
        out[i] = arrived[0][i] + part[0] if arrived else part[0]


def collect(index, keep, got, before, *arrived):
    shape = (2,) + keep.shape[1:]
    one = pl.BlockSpec((1,) + shape[1:], lambda i: (index, 0, 0))
    whole = pl.BlockSpec(shape, lambda i: (0, 0, 0))
    return pl.pallas_call(
        collect_kernel,
        grid=(1,),
        in_specs=[one, one] + [whole] * len(arrived) + [pl.BlockSpec(memory_space=pl.ANY)],
        out_specs=whole,
        out_shape=jax.ShapeDtypeStruct(shape, jnp.float32),
        compiler_params=pltpu.CompilerParams(vmem_limit_bytes=SMALL_VMEM),
        name="collect",
    )(keep, got, *arrived, before)


def exchange_lanes(tiles):
    lane = lax.broadcasted_iota(jnp.int32, tiles[0].shape, 1) // BLOCK
    for bit in (1, 2, 4):
        upper = (lane // bit) % 2 == 1
        out = list(tiles)
        for a in range(8):
            if a & bit:
                continue
            x, y = tiles[a], tiles[a | bit]
            if bit == 4:
                moved = pltpu.roll(jnp.where(upper, x, y), LANES // 2, 1)
                out[a], out[a | bit] = jnp.where(upper, moved, x), jnp.where(upper, y, moved)
                continue
            out[a] = jnp.where(upper, pltpu.roll(y, BLOCK * bit, 1), x)
            out[a | bit] = jnp.where(upper, y, pltpu.roll(x, LANES - BLOCK * bit, 1))
        tiles = out
    return tiles


def ring_total(refs, half, start, size=BLOCK):
    own, late, early, got_late, got_early = refs
    at = pl.ds(start, size)
    if half:
        return own[1, at] + early[0, at] + got_late[at]
    return own[0, at] + late[0, at] + got_early[at]


def direct_kernel(*refs):
    keep, give = refs[6:]
    yl = lax.axis_index("yl")
    rows = keep.shape[0] // 2
    for half in range(2):
        for a in range(rows):
            for h, dst in ((yl, keep), (1 - yl, give)):
                start = pl.multiple_of(BLOCK * (rows * h + a), BLOCK)
                dst[rows * half + a] = ring_total(refs[:5], half, start)


def turn_blocks(x):
    turned = x.T
    out = jnp.zeros(x.shape, x.dtype)
    for a in range(8):
        block = jnp.concatenate(
            [turned[BLOCK * a : BLOCK * (a + 1)], jnp.zeros((BLOCK, LANES - BLOCK), x.dtype)],
            axis=1,
        )
        out = out + (pltpu.roll(block, BLOCK * a, 1) if a else block)
    return out


def mail_kernel(*refs):
    mail = refs[5]
    zi = lax.axis_index("z")
    groups = mail.shape[1]
    rows = 4 * groups
    across = lax.broadcasted_iota(jnp.int32, (BLOCK, LANES), 1) % BLOCK
    down = lax.broadcasted_iota(jnp.int32, (BLOCK, LANES), 0)

    for g in range(groups):
        firsts = []
        for h in range(2):
            tiles = [
                ring_total(refs[:5], row // rows, BLOCK * (rows * h + row % rows))
                for row in range(8 * g, 8 * g + 8)
            ]
            swapped = exchange_lanes(tiles)
            firsts.append(swapped[0])
            for m in range(1, 8):
                mail[lax.rem(zi + 8 * h + m, 16), g] = swapped[m]
        middle = 0.0
        for half in range(2):
            if rows * half < 8 * g + 8 and rows * (half + 1) > 8 * g:
                place = 2 * rows * BLOCK + g - rows * half // 8
                middle = middle + ring_total(refs[:5], half, place, 1)
        for at, below, above in ((8, firsts[0], firsts[1]), (0, firsts[1], firsts[0])):
            mail[zi + at, g] = jnp.where(
                across < down, below, jnp.where(across == down, middle, turn_blocks(above))
            )


def pack(rows, *sums):
    whole = pl.BlockSpec(memory_space=pltpu.VMEM)

    def call(kernel, shapes, name, *before):
        return pl.pallas_call(
            kernel,
            in_specs=[whole] * 5 + [pl.BlockSpec(memory_space=pl.ANY)] * len(before),
            out_specs=[whole] * len(shapes),
            out_shape=[jax.ShapeDtypeStruct(s, jnp.float32) for s in shapes],
            compiler_params=pltpu.CompilerParams(vmem_limit_bytes=SMALL_VMEM),
            name=name,
        )(*sums, *before)

    (mail,) = call(mail_kernel, [(16, rows // 8, BLOCK, LANES)], "mail")
    keep, give = call(direct_kernel, [(rows, BLOCK, LANES)] * 2, "direct", mail)
    return keep, give, mail


def join_kernel(keep, got, mail, out):
    zi = lax.axis_index("z")
    groups = mail.shape[1]
    lane = lax.broadcasted_iota(jnp.int32, (BLOCK, LANES), 1)
    level = lax.broadcasted_iota(jnp.int32, (BLOCK, LANES), 0)
    rest = jnp.zeros((BLOCK, LANES - BLOCK), jnp.float32)
    for g in range(groups):
        stack = []
        for k in range(8):
            z = lax.rem(zi + k, 8)
            stack.append(mail[z, g] + mail[z + 8, g])
        turned = jnp.concatenate(stack, axis=0).T.reshape(8, BLOCK, LANES)
        tiles = [keep[8 * g + a] + got[8 * g + a] for a in range(8)]
        packed = jnp.where(lane < BLOCK, tiles[0], 0.0)
        for a in range(1, 8):
            packed = packed + pltpu.roll(jnp.where(lane < BLOCK, tiles[a], 0.0), BLOCK * a, 1)
        upper = packed.T
        direct = jnp.stack(
            [
                jnp.where(
                    lane < level,
                    jnp.concatenate([upper[BLOCK * a : BLOCK * (a + 1)], rest], axis=1),
                    tiles[a],
                )
                for a in range(8)
            ]
        )
        out[:, 8 * g : 8 * g + 8, :LANES] = jnp.swapaxes(direct, 0, 1)
        out[:, 8 * g : 8 * g + 8, LANES:] = jnp.swapaxes(turned, 0, 1)


def join(keep, got, mail):
    groups = mail.shape[1]
    whole = pl.BlockSpec(memory_space=pltpu.VMEM)
    return pl.pallas_call(
        join_kernel,
        in_specs=[whole] * 3,
        out_specs=whole,
        out_shape=jax.ShapeDtypeStruct((BLOCK, 8 * groups, 2 * LANES), jnp.float32),
        compiler_params=pltpu.CompilerParams(vmem_limit_bytes=SMALL_VMEM),
        name="join",
    )(keep, got, mail)


def transform_kernel(basis, data, relabel, out):
    dot = functools.partial(jnp.dot, preferred_element_type=jnp.float32)
    x = data[...]
    high = x.astype(jnp.bfloat16)
    low = (x - high.astype(jnp.float32)).astype(jnp.bfloat16)
    high = dot(high, relabel[...]).astype(jnp.bfloat16)
    low = dot(low, relabel[...]).astype(jnp.bfloat16)
    out[...] = dot(basis[0], high) + (dot(basis[0], low) + dot(basis[1], high))


def transform(basis, data, relabel):
    whole = pl.BlockSpec(memory_space=pltpu.VMEM)
    return pl.pallas_call(
        transform_kernel,
        in_specs=[whole] * 3,
        out_specs=whole,
        out_shape=jax.ShapeDtypeStruct((basis.shape[1], data.shape[1]), jnp.float32),
        compiler_params=pltpu.CompilerParams(vmem_limit_bytes=SMALL_VMEM),
        name="transform",
    )(basis, data, relabel)


def update_kernel(events, inside, traces, older, data, out):
    count = older.shape[0]
    for t in range(count):
        old = older[t].astype(jnp.float32)
        moved = old + step_weight * events[t] * (
            data[t].astype(jnp.float32) - old - traces[:, t, :]
        )
        size = jnp.maximum(jnp.abs(moved) - shrink_level, 0.0)
        shrunk = jnp.where(moved < 0.0, -size, size)
        out[t] = jnp.where(inside[t] > 0, shrunk, 0.0).astype(jnp.bfloat16)


def update(events, inside, traces, older, data):
    whole = pl.BlockSpec(memory_space=pltpu.VMEM)
    scalars = pl.BlockSpec(memory_space=pltpu.SMEM)
    return pl.pallas_call(
        update_kernel,
        in_specs=[scalars, scalars, whole, whole, whole],
        out_specs=whole,
        out_shape=jax.ShapeDtypeStruct(older.shape, jnp.bfloat16),
        compiler_params=pltpu.CompilerParams(vmem_limit_bytes=SMALL_VMEM),
        name="update",
    )(events, inside, traces, older, data)


def slot_windows(slots, window_lengths, capacity):
    starts = jnp.cumsum(window_lengths) - window_lengths
    window = slots // capacity
    offset = slots % capacity
    select = window[:, None] == jnp.arange(window_lengths.shape[0], dtype=jnp.int32)[None, :]
    begin = jnp.sum(jnp.where(select, starts[None, :], 0), axis=1)
    length = jnp.sum(jnp.where(select, window_lengths[None, :], 0), axis=1)
    return begin + offset, offset < length


def time_basis(times, inside, freqs):
    phase = times[:, None] * freqs[None, :] % NT
    angle = phase.astype(jnp.float32) * (2.0 * math.pi / NT)
    scale = jnp.where(inside, 1.0 / math.sqrt(F), 0.0).astype(jnp.float32)[:, None]
    odd = (jnp.arange(freqs.shape[0]) % 2 == 1)[None, :]
    return jnp.where(odd, -jnp.sin(angle), jnp.cos(angle)) * scale


def ring(n, d):
    return [(i, (i + d) % n) for i in range(n)]


def other_half_kernel(arrived, before, out):
    out[...] = arrived[1]


def other_half(arrived, before):
    whole = pl.BlockSpec(memory_space=pltpu.VMEM)
    return pl.pallas_call(
        other_half_kernel,
        in_specs=[whole, pl.BlockSpec(memory_space=pl.ANY)],
        out_specs=whole,
        out_shape=jax.ShapeDtypeStruct(arrived.shape[1:], arrived.dtype),
        compiler_params=pltpu.CompilerParams(vmem_limit_bytes=SMALL_VMEM),
        name="other_half",
    )(arrived, before)


def lift_kernel(source, out, sem):
    copy = pltpu.make_async_copy(source, out, sem)
    copy.start()
    copy.wait()


def lift(source):
    return pl.pallas_call(
        lift_kernel,
        in_specs=[pl.BlockSpec(memory_space=pl.ANY)],
        out_specs=pl.BlockSpec(memory_space=pltpu.VMEM),
        out_shape=jax.ShapeDtypeStruct(source.shape, source.dtype),
        scratch_shapes=[pltpu.SemaphoreType.DMA],
        compiler_params=pltpu.CompilerParams(vmem_limit_bytes=SMALL_VMEM),
        cost_estimate=pl.CostEstimate(
            flops=0, bytes_accessed=8 * source.size, transcendentals=0
        ),
        name="lift",
    )(source)


def ring_sums(keep_first, keep, give_first, give):
    swap = functools.partial(lax.ppermute, axis_name="core", perm=ring(2, 1))
    step = functools.partial(
        lax.ppermute,
        axis_name=("core", "z"),
        perm=[
            (c * RING + z, c * RING + (z + (1 if c == 0 else -1)) % RING)
            for c in range(2)
            for z in range(RING)
        ],
    )
    payload = collect(0, lift(keep_first), swap(give_first), keep_first)
    payload, give = lax.optimization_barrier((payload, give))
    got = swap(give)
    flying = [step(payload)]
    for n in range(6):
        payload = collect(n, keep, got, payload, *flying[:-1])
        flying = flying[-1:] + [step(payload)]
    early, late = flying
    return late, early, swap(late[1]), swap(other_half(early, payload))


def on_device(
    spectra, primaries, wavelet_ratio, window_lengths, event_mask, pairing, old_traces, data_traces
):
    src = ("yl", "z")
    freq = ("x", "yh", "core")
    freq_count = lax.axis_size(freq)
    freq_dev = spectra.shape[0]
    width = spectra.shape[2]
    capacity = old_traces.shape[0]
    yl, zi = lax.axis_index("yl"), lax.axis_index("z")
    own = yl * 8 + zi
    lanes = jnp.arange(width, dtype=jnp.int32)
    blocks = lanes // BLOCK
    ids = jnp.arange(pairing.shape[0], dtype=jnp.int32)

    def paired(block):
        return jnp.sum(jnp.where(block[:, None] == ids[None, :], pairing[None, :], 0), axis=1)

    target = paired((blocks + own) % pairing.shape[0]) * BLOCK + lanes % BLOCK
    restore = (target[:, None] == lanes[None, :]).astype(jnp.bfloat16)
    slots = jnp.arange(capacity * freq_count, dtype=jnp.int32)
    times, inside = slot_windows(slots, window_lengths, capacity)
    basis = time_basis(
        times, inside, jnp.arange(2 * freq_dev * freq_count, dtype=jnp.int32) // 2
    )
    coarse = lax.reduce_precision(basis, 8, 7)
    basis = jnp.stack([coarse, basis - coarse]).astype(jnp.bfloat16)
    own_slots = lax.axis_index(freq) * capacity + jnp.arange(capacity, dtype=jnp.int32)
    _, inside_own = slot_windows(own_slots, window_lengths, capacity)

    *sends, ends = product(spectra, primaries, wavelet_ratio, pairing)
    keep, give, mail = pack(2 * freq_dev, ends, *ring_sums(*sends))
    got = lax.ppermute(give, "yl", ring(2, 1))
    mail = lax.all_to_all(mail, src, split_axis=0, concat_axis=0, tiled=True)
    whole = join(keep, got, mail)
    spread = lax.all_to_all(whole, freq, split_axis=0, concat_axis=0, tiled=True)
    slotted = transform(basis, spread.reshape(-1, width), restore)
    slotted = slotted.reshape(freq_count, capacity, width)
    traces = lax.all_to_all(slotted, freq, split_axis=0, concat_axis=0, tiled=True)
    return update(
        event_mask.astype(jnp.float32),
        inside_own.astype(jnp.int32),
        traces,
        old_traces,
        data_traces,
    )


def solution(mesh):
    shape = tuple(mesh.shape.values())
    cores = 2 if shape[0] % 2 == 0 else 1
    yh = 2 if shape[0] % 4 == 0 else 1
    devices = mesh.devices.reshape(shape[0] // (cores * yh), yh, cores, shape[1] // 8, 8)
    split = Mesh(devices, ("x", "yh", "core", "yl", "z"))
    freq = ("x", "yh", "core")
    src = ("yl", "z")
    in_specs = (
        P(freq, None, None, src),
        P(freq, None, src, None),
        P(None, freq),
        P(),
        P(freq),
        P(),
        P(freq, src, None),
        P(freq, src, None),
    )
    return jax.shard_map(
        on_device, mesh=split, in_specs=in_specs, out_specs=P(freq, src, None), check_vma=False
    )
```

```python
import functools
import math

import jax
import jax.numpy as jnp
from jax import lax
from jax.experimental import pallas as pl
from jax.experimental.pallas import tpu as pltpu
from jax.sharding import Mesh, PartitionSpec as P

F = 192
NT = 384
LANES = 128
BLOCK = 16
RING = 8
PRODUCT_VMEM = 59 * 1024 * 1024
SMALL_VMEM = 24 * 1024 * 1024

shrink_level = 0.25
step_weight = 0.5


def window(near, far, shift):
    lane = lax.broadcasted_iota(jnp.int32, near.shape, 1)
    row = lax.broadcasted_iota(jnp.int32, near.shape, 0)
    if shift:
        near = pltpu.roll(near, LANES - shift, 1)
        far = pltpu.roll(far, LANES - shift, 1)
    return jnp.where((lane < LANES - shift) & (lane >= row), near, far)


def product_kernel(
    pairing, ratio, spectra, primaries, keep_first, keep, give_first, give, own,
    left, right, relabel, relabel_low, chosen, held, out, slots, left_sems, right_sems, out_sems,
):
    freqs, _, width, depth = left.shape
    count = freqs // 2
    half = width // 2
    rows = 2 * count
    tail = 2 * rows * BLOCK
    core, zi = lax.axis_index("core"), lax.axis_index("z")
    lane = lax.broadcasted_iota(jnp.int32, (BLOCK, LANES), 1)
    level = lax.broadcasted_iota(jnp.int32, (BLOCK, LANES), 0)

    def fetch_left(i):
        return pltpu.make_async_copy(spectra.at[i], left.at[i], left_sems.at[i])

    def fetch_right(i):
        return pltpu.make_async_copy(primaries.at[i], right.at[i], right_sems.at[i])

    for i in range(freqs):
        fetch_right(i).start()
        fetch_left(i).start()
    block = lax.broadcasted_iota(jnp.int32, (8, width), 1) // BLOCK
    source = jnp.zeros((8, width), jnp.int32)
    for b in range(width // BLOCK):
        source = jnp.where(block == b, pairing[b], source)
    source = source * BLOCK + lax.broadcasted_iota(jnp.int32, (8, width), 1) % BLOCK
    for r in range(0, width, 8):
        row = lax.broadcasted_iota(jnp.int32, (8, width), 0) + r
        relabel[r : r + 8] = jnp.where(row == source, 1.0, 0.0)
    relabel_low[...] = relabel[...].astype(jnp.bfloat16)
    out[:, tail:] = jnp.zeros((out.shape[0], out.shape[1] - tail, LANES), out.dtype)
    for second in range(2):
        long_up = second == core
        for t in range(RING):
            k = lax.rem(t - zi + RING, RING)
            away = jnp.where(k <= 4, 4 - k, k - 4)
            goes_up = (k < 4) | ((k == 4) & long_up)
            send = 2 * away - jnp.where(long_up == goes_up, 0, 1)
            mine = goes_up == (core == 0)
            slots[second, t] = jnp.where(k == 0, 14 + second, send + jnp.where(mine, 0, 7))

    def cut(i):
        second = lax.div(i, count)
        real, imag = held[i & 1, 0], held[i & 1, 1]
        real = 0.5 * (real + real.T)
        imag = 0.5 * (imag + imag.T)
        wr = ratio[0, i]
        wi = ratio[1, i]
        for c, z in enumerate((wr * real - wi * imag, wr * imag + wi * real)):
            row = 2 * i + c
            shift = row & 7
            place = tail + (row >> 3) - second * (2 * count // 8)
            row = row - second * rows
            for t in range(RING):
                k = slots[second, t]
                low = z[BLOCK * t : BLOCK * (t + 1)]
                high = z[half + BLOCK * t : half + BLOCK * (t + 1)]
                out[k, pl.ds(pl.multiple_of(row * BLOCK, BLOCK), BLOCK)] = window(
                    low[:, :half], low[:, half:], BLOCK * t
                )
                out[k, pl.ds(pl.multiple_of((rows + row) * BLOCK, BLOCK), BLOCK)] = window(
                    high[:, half:], high[:, :half], BLOCK * t
                )
                middle = jnp.where(lane == level + BLOCK * t, low[:, half:], 0.0)
                middle = jnp.sum(middle, axis=0, keepdims=True)
                middle = pltpu.roll(middle, (BLOCK * (shift - t)) & (LANES - 1), 1)
                out[k, pl.ds(place, 1)] += middle

    def multiply(i):
        a = left[i].reshape(2 * width, depth)
        by_real = jnp.dot(a, chosen[i & 1, 0], preferred_element_type=jnp.float32)
        by_imag = jnp.dot(a, chosen[i & 1, 1], preferred_element_type=jnp.float32)
        held[i & 1, 0] = by_real[:width] - by_imag[width:]
        held[i & 1, 1] = by_imag[:width] + by_real[width:]

    def choose(i):
        for b in range(2):
            chosen[i & 1, b] = jnp.dot(
                right[i, b], relabel_low[...], preferred_element_type=jnp.float32
            ).astype(jnp.bfloat16)

    def stages(i, carry):
        fetch_right(i).wait()
        fetch_left(i - 1).wait()
        cut(i - 2)
        multiply(i - 1)
        choose(i)
        return carry

    def copies(moves):
        return [
            pltpu.make_async_copy(out.at[slot], dst.at[i], out_sems.at[slot])
            for slot, dst, i in moves
        ]

    early = copies(
        [(0, keep_first, 0)]
        + [(n, keep, n - 1) for n in (2, 4, 6)]
        + [(7 + n, give, n - 1) for n in (1, 3, 5)]
        + [(14, own, 0)]
    )
    late = copies(
        [(7, give_first, 0)]
        + [(n, keep, n - 1) for n in (1, 3, 5)]
        + [(7 + n, give, n - 1) for n in (2, 4, 6)]
        + [(15, own, 1)]
    )
    fetch_right(0).wait()
    choose(0)
    fetch_right(1).wait()
    fetch_left(0).wait()
    multiply(0)
    choose(1)
    lax.fori_loop(2, count + 2, stages, 0)
    for copy in early:
        copy.start()
    lax.fori_loop(count + 2, freqs, stages, 0)
    fetch_left(freqs - 1).wait()
    cut(freqs - 2)
    multiply(freqs - 1)
    cut(freqs - 1)
    for copy in late:
        copy.start()
    for copy in early + late:
        copy.wait()


def product(spectra, primaries, ratio, pairing):
    freqs = spectra.shape[0]
    width, depth = spectra.shape[2:]
    height = 2 * freqs * BLOCK + 8
    smem = pl.BlockSpec(memory_space=pltpu.SMEM)
    anywhere = pl.BlockSpec(memory_space=pl.ANY)
    shapes = [(n, height, LANES) for n in (1, 6, 1, 6, 2)]
    return pl.pallas_call(
        product_kernel,
        in_specs=[smem, smem, anywhere, anywhere],
        out_specs=[anywhere] * 5,
        out_shape=[jax.ShapeDtypeStruct(s, jnp.float32) for s in shapes],
        scratch_shapes=[
            pltpu.VMEM(spectra.shape, spectra.dtype),
            pltpu.VMEM(primaries.shape, primaries.dtype),
            pltpu.VMEM((width, width), jnp.float32),
            pltpu.VMEM((width, width), jnp.bfloat16),
            pltpu.VMEM((2, 2, depth, width), jnp.bfloat16),
            pltpu.VMEM((2, 2, width, width), jnp.float32),
            pltpu.VMEM((16, height, LANES), jnp.float32),
            pltpu.SMEM((2, RING), jnp.int32),
            pltpu.SemaphoreType.DMA((freqs,)),
            pltpu.SemaphoreType.DMA((freqs,)),
            pltpu.SemaphoreType.DMA((16,)),
        ],
        compiler_params=pltpu.CompilerParams(vmem_limit_bytes=PRODUCT_VMEM),
        cost_estimate=pl.CostEstimate(
            flops=freqs * 2 * 2 * width * 2 * width * depth,
            bytes_accessed=freqs * 8 * width * depth + 16 * height * LANES * 4,
            transcendentals=0,
        ),
        name="product",
    )(pairing, ratio, spectra, primaries)


def collect_kernel(arrivals, keep, got, *refs):
    arrived, outs = refs[:arrivals], refs[arrivals + 1 :]
    outs = outs if len(outs) == 2 else (outs[0].at[pl.ds(0, 1)], outs[0].at[pl.ds(1, 1)])
    for i, part in enumerate((keep, got)):
        outs[i][0] = arrived[0][i] + part[0] if arrived else part[0]


def collect(index, keep, got, before, *arrived, split=False):
    shape = (2,) + keep.shape[1:]
    one = pl.BlockSpec((1,) + shape[1:], lambda i: (index, 0, 0))
    whole = pl.BlockSpec(shape, lambda i: (0, 0, 0))
    half = pl.BlockSpec((1,) + shape[1:], lambda i: (0, 0, 0))
    return pl.pallas_call(
        functools.partial(collect_kernel, len(arrived)),
        grid=(1,),
        in_specs=[one, one] + [whole] * len(arrived) + [pl.BlockSpec(memory_space=pl.ANY)],
        out_specs=[half, half] if split else whole,
        out_shape=[jax.ShapeDtypeStruct((1,) + shape[1:], jnp.float32)] * 2
        if split
        else jax.ShapeDtypeStruct(shape, jnp.float32),
        compiler_params=pltpu.CompilerParams(vmem_limit_bytes=SMALL_VMEM),
        name="collect",
    )(keep, got, *arrived, before)


def exchange_lanes(tiles):
    lane = lax.broadcasted_iota(jnp.int32, tiles[0].shape, 1) // BLOCK
    for bit in (1, 2, 4):
        upper = (lane // bit) % 2 == 1
        out = list(tiles)
        for a in range(8):
            if a & bit:
                continue
            x, y = tiles[a], tiles[a | bit]
            if bit == 4:
                moved = pltpu.roll(jnp.where(upper, x, y), LANES // 2, 1)
                out[a], out[a | bit] = jnp.where(upper, moved, x), jnp.where(upper, y, moved)
                continue
            out[a] = jnp.where(upper, pltpu.roll(y, BLOCK * bit, 1), x)
            out[a | bit] = jnp.where(upper, y, pltpu.roll(x, LANES - BLOCK * bit, 1))
        tiles = out
    return tiles


def ring_total(refs, half, start, size=BLOCK):
    own, late, early, got_late, got_early = refs
    at = pl.ds(start, size)
    if half:
        return own[1, at] + early[0, at] + got_late[at]
    return own[0, at] + late[0, at] + got_early[at]


def direct_kernel(*refs):
    keep, give = refs[6:]
    yl = lax.axis_index("yl")
    rows = keep.shape[0] // 2
    for half in range(2):
        for a in range(rows):
            for h, dst in ((yl, keep), (1 - yl, give)):
                start = pl.multiple_of(BLOCK * (rows * h + a), BLOCK)
                dst[rows * half + a] = ring_total(refs[:5], half, start)


def mail_kernel(*refs):
    mail = refs[5]
    zi = lax.axis_index("z")
    groups = mail.shape[1]
    rows = 4 * groups
    across = lax.broadcasted_iota(jnp.int32, (BLOCK, LANES), 1) % BLOCK
    down = lax.broadcasted_iota(jnp.int32, (BLOCK, LANES), 0)

    for g in range(groups):
        firsts = []
        for h in range(2):
            tiles = [
                ring_total(refs[:5], row // rows, BLOCK * (rows * h + row % rows))
                for row in range(8 * g, 8 * g + 8)
            ]
            swapped = exchange_lanes(tiles)
            firsts.append(swapped[0])
            for m in range(1, 8):
                mail[lax.rem(zi + 8 * h + m, 16), g] = swapped[m]
        middle = 0.0
        for half in range(2):
            if rows * half < 8 * g + 8 and rows * (half + 1) > 8 * g:
                place = 2 * rows * BLOCK + g - rows * half // 8
                middle = middle + ring_total(refs[:5], half, place, 1)
        for at, below in ((8, firsts[0]), (0, firsts[1])):
            mail[zi + at, g] = jnp.where(across == down, middle, below)


def pack(rows, *sums):
    whole = pl.BlockSpec(memory_space=pltpu.VMEM)

    def call(kernel, shapes, name, *before):
        return pl.pallas_call(
            kernel,
            in_specs=[whole] * 5 + [pl.BlockSpec(memory_space=pl.ANY)] * len(before),
            out_specs=[whole] * len(shapes),
            out_shape=[jax.ShapeDtypeStruct(s, jnp.float32) for s in shapes],
            compiler_params=pltpu.CompilerParams(vmem_limit_bytes=SMALL_VMEM),
            name=name,
        )(*sums, *before)

    (mail,) = call(mail_kernel, [(16, rows // 8, BLOCK, LANES)], "mail")
    keep, give = call(direct_kernel, [(rows, BLOCK, LANES)] * 2, "direct", mail)
    return keep, give, mail


def join_kernel(keep, got, mail, out):
    zi = lax.axis_index("z")
    groups = mail.shape[1]
    lane = lax.broadcasted_iota(jnp.int32, (BLOCK, LANES), 1)
    level = lax.broadcasted_iota(jnp.int32, (BLOCK, LANES), 0)
    rest = jnp.zeros((BLOCK, LANES - BLOCK), jnp.float32)
    for g in range(groups):
        stack = []
        for k in range(8):
            z = lax.rem(zi + k, 8)
            stack.append(mail[z, g] + mail[z + 8, g])
        turned = jnp.concatenate(stack, axis=0).T.reshape(8, BLOCK, LANES)
        tiles = [keep[8 * g + a] + got[8 * g + a] for a in range(8)]
        packed = jnp.where(lane < BLOCK, tiles[0], 0.0)
        for a in range(1, 8):
            packed = packed + pltpu.roll(jnp.where(lane < BLOCK, tiles[a], 0.0), BLOCK * a, 1)
        upper = packed.T
        own = lane < level
        direct = [
            jnp.where(
                own, jnp.concatenate([upper[BLOCK * a : BLOCK * (a + 1)], rest], axis=1), tiles[a]
            )
            for a in range(8)
        ]
        mirrored = [jnp.where(own, tiles[a], turned[a]) for a in range(8)]
        out[:, 8 * g : 8 * g + 8, :LANES] = jnp.swapaxes(jnp.stack(direct), 0, 1)
        out[:, 8 * g : 8 * g + 8, LANES:] = jnp.swapaxes(jnp.stack(mirrored), 0, 1)


def join(keep, got, mail):
    groups = mail.shape[1]
    whole = pl.BlockSpec(memory_space=pltpu.VMEM)
    return pl.pallas_call(
        join_kernel,
        in_specs=[whole] * 3,
        out_specs=whole,
        out_shape=jax.ShapeDtypeStruct((BLOCK, 8 * groups, 2 * LANES), jnp.float32),
        compiler_params=pltpu.CompilerParams(vmem_limit_bytes=SMALL_VMEM),
        name="join",
    )(keep, got, mail)


def transform_kernel(basis, data, relabel, out):
    dot = functools.partial(jnp.dot, preferred_element_type=jnp.float32)
    x = data[...]
    high = x.astype(jnp.bfloat16)
    low = (x - high.astype(jnp.float32)).astype(jnp.bfloat16)
    high = dot(high, relabel[...]).astype(jnp.bfloat16)
    low = dot(low, relabel[...]).astype(jnp.bfloat16)
    out[...] = dot(basis[0], high) + (dot(basis[0], low) + dot(basis[1], high))


def transform(basis, data, relabel):
    whole = pl.BlockSpec(memory_space=pltpu.VMEM)
    return pl.pallas_call(
        transform_kernel,
        in_specs=[whole] * 3,
        out_specs=whole,
        out_shape=jax.ShapeDtypeStruct((basis.shape[1], data.shape[1]), jnp.float32),
        compiler_params=pltpu.CompilerParams(vmem_limit_bytes=SMALL_VMEM),
        name="transform",
    )(basis, data, relabel)


def update_kernel(events, inside, traces, older, data, out):
    count = older.shape[0]
    for t in range(count):
        old = older[t].astype(jnp.float32)
        moved = old + step_weight * events[t] * (
            data[t].astype(jnp.float32) - old - traces[:, t, :]
        )
        size = jnp.maximum(jnp.abs(moved) - shrink_level, 0.0)
        shrunk = jnp.where(moved < 0.0, -size, size)
        out[t] = jnp.where(inside[t] > 0, shrunk, 0.0).astype(jnp.bfloat16)


def update(events, inside, traces, older, data):
    whole = pl.BlockSpec(memory_space=pltpu.VMEM)
    scalars = pl.BlockSpec(memory_space=pltpu.SMEM)
    return pl.pallas_call(
        update_kernel,
        in_specs=[scalars, scalars, whole, whole, whole],
        out_specs=whole,
        out_shape=jax.ShapeDtypeStruct(older.shape, jnp.bfloat16),
        compiler_params=pltpu.CompilerParams(vmem_limit_bytes=SMALL_VMEM),
        name="update",
    )(events, inside, traces, older, data)


def slot_windows(slots, window_lengths, capacity):
    starts = jnp.cumsum(window_lengths) - window_lengths
    window = slots // capacity
    offset = slots % capacity
    select = window[:, None] == jnp.arange(window_lengths.shape[0], dtype=jnp.int32)[None, :]
    begin = jnp.sum(jnp.where(select, starts[None, :], 0), axis=1)
    length = jnp.sum(jnp.where(select, window_lengths[None, :], 0), axis=1)
    return begin + offset, offset < length


def time_basis(times, inside, freqs):
    phase = times[:, None] * freqs[None, :] % NT
    angle = phase.astype(jnp.float32) * (2.0 * math.pi / NT)
    scale = jnp.where(inside, 1.0 / math.sqrt(F), 0.0).astype(jnp.float32)[:, None]
    odd = (jnp.arange(freqs.shape[0]) % 2 == 1)[None, :]
    return jnp.where(odd, -jnp.sin(angle), jnp.cos(angle)) * scale


def ring(n, d):
    return [(i, (i + d) % n) for i in range(n)]


def other_half_kernel(arrived, before, out):
    out[...] = arrived[1]


def other_half(arrived, before):
    whole = pl.BlockSpec(memory_space=pltpu.VMEM)
    return pl.pallas_call(
        other_half_kernel,
        in_specs=[whole, pl.BlockSpec(memory_space=pl.ANY)],
        out_specs=whole,
        out_shape=jax.ShapeDtypeStruct(arrived.shape[1:], arrived.dtype),
        compiler_params=pltpu.CompilerParams(vmem_limit_bytes=SMALL_VMEM),
        name="other_half",
    )(arrived, before)


def lift_kernel(source, out, sem):
    copy = pltpu.make_async_copy(source, out, sem)
    copy.start()
    copy.wait()


def lift(source):
    return pl.pallas_call(
        lift_kernel,
        in_specs=[pl.BlockSpec(memory_space=pl.ANY)],
        out_specs=pl.BlockSpec(memory_space=pltpu.VMEM),
        out_shape=jax.ShapeDtypeStruct(source.shape, source.dtype),
        scratch_shapes=[pltpu.SemaphoreType.DMA],
        compiler_params=pltpu.CompilerParams(vmem_limit_bytes=SMALL_VMEM),
        cost_estimate=pl.CostEstimate(
            flops=0, bytes_accessed=8 * source.size, transcendentals=0
        ),
        name="lift",
    )(source)


def ring_sums(keep_first, keep, give_first, give):
    swap = functools.partial(lax.ppermute, axis_name="core", perm=ring(2, 1))
    step = functools.partial(
        lax.ppermute,
        axis_name=("core", "z"),
        perm=[
            (c * RING + z, c * RING + (z + (1 if c == 0 else -1)) % RING)
            for c in range(2)
            for z in range(RING)
        ],
    )
    cross = functools.partial(
        lax.ppermute,
        axis_name=("core", "z"),
        perm=[
            (c * RING + z, (1 - c) * RING + (z + (1 if c == 0 else -1)) % RING)
            for c in range(2)
            for z in range(RING)
        ],
    )
    payload = collect(0, lift(keep_first), swap(give_first), keep_first)
    payload, give = lax.optimization_barrier((payload, give))
    got = swap(give)
    flying = [step(payload)]
    for n in range(5):
        payload = collect(n, keep, got, payload, *flying[:-1])
        flying = flying[-1:] + [step(payload)]
    mine, other = collect(5, keep, got, payload, flying[0], split=True)
    return step(mine), flying[1], cross(other)[0], swap(other_half(flying[1], other))


def on_device(
    spectra, primaries, wavelet_ratio, window_lengths, event_mask, pairing, old_traces, data_traces
):
    src = ("yl", "z")
    freq = ("x", "yh", "core")
    freq_count = lax.axis_size(freq)
    freq_dev = spectra.shape[0]
    width = spectra.shape[2]
    capacity = old_traces.shape[0]
    yl, zi = lax.axis_index("yl"), lax.axis_index("z")
    own = yl * 8 + zi
    lanes = jnp.arange(width, dtype=jnp.int32)
    blocks = lanes // BLOCK
    ids = jnp.arange(pairing.shape[0], dtype=jnp.int32)

    def paired(block):
        return jnp.sum(jnp.where(block[:, None] == ids[None, :], pairing[None, :], 0), axis=1)

    target = paired((blocks + own) % pairing.shape[0]) * BLOCK + lanes % BLOCK
    restore = (target[:, None] == lanes[None, :]).astype(jnp.bfloat16)
    slots = jnp.arange(capacity * freq_count, dtype=jnp.int32)
    times, inside = slot_windows(slots, window_lengths, capacity)
    basis = time_basis(
        times, inside, jnp.arange(2 * freq_dev * freq_count, dtype=jnp.int32) // 2
    )
    coarse = lax.reduce_precision(basis, 8, 7)
    basis = jnp.stack([coarse, basis - coarse]).astype(jnp.bfloat16)
    own_slots = lax.axis_index(freq) * capacity + jnp.arange(capacity, dtype=jnp.int32)
    _, inside_own = slot_windows(own_slots, window_lengths, capacity)

    *sends, ends = product(spectra, primaries, wavelet_ratio, pairing)
    keep, give, mail = pack(2 * freq_dev, ends, *ring_sums(*sends))
    got = lax.ppermute(give, "yl", ring(2, 1))
    mail = lax.all_to_all(mail, src, split_axis=0, concat_axis=0, tiled=True)
    whole = join(keep, got, mail)
    spread = lax.all_to_all(whole, freq, split_axis=0, concat_axis=0, tiled=True)
    slotted = transform(basis, spread.reshape(-1, width), restore)
    slotted = slotted.reshape(freq_count, capacity, width)
    traces = lax.all_to_all(slotted, freq, split_axis=0, concat_axis=0, tiled=True)
    return update(
        event_mask.astype(jnp.float32),
        inside_own.astype(jnp.int32),
        traces,
        old_traces,
        data_traces,
    )


def solution(mesh):
    shape = tuple(mesh.shape.values())
    cores = 2 if shape[0] % 2 == 0 else 1
    yh = 2 if shape[0] % 4 == 0 else 1
    devices = mesh.devices.reshape(shape[0] // (cores * yh), yh, cores, shape[1] // 8, 8)
    split = Mesh(devices, ("x", "yh", "core", "yl", "z"))
    freq = ("x", "yh", "core")
    src = ("yl", "z")
    in_specs = (
        P(freq, None, None, src),
        P(freq, None, src, None),
        P(None, freq),
        P(),
        P(freq),
        P(),
        P(freq, src, None),
        P(freq, src, None),
    )
    return jax.shard_map(
        on_device, mesh=split, in_specs=in_specs, out_specs=P(freq, src, None), check_vma=False
    )
```

```python
import functools
import math

import jax
import jax.numpy as jnp
from jax import lax
from jax.experimental import pallas as pl
from jax.experimental.pallas import tpu as pltpu
from jax.sharding import Mesh, PartitionSpec as P

F = 192
NT = 384
LANES = 128
BLOCK = 16
RING = 8
PRODUCT_VMEM = 59 * 1024 * 1024
SMALL_VMEM = 24 * 1024 * 1024

shrink_level = 0.25
step_weight = 0.5


def window(near, far, shift):
    lane = lax.broadcasted_iota(jnp.int32, near.shape, 1)
    row = lax.broadcasted_iota(jnp.int32, near.shape, 0)
    if shift:
        near = pltpu.roll(near, LANES - shift, 1)
        far = pltpu.roll(far, LANES - shift, 1)
    return jnp.where((lane < LANES - shift) & (lane >= row), near, far)


def product_kernel(
    pairing, ratio, spectra, primaries, keep_first, keep, keep_last, give_first, give, give_last, own,
    left, right, relabel, relabel_low, chosen, held, out, slots, left_sems, right_sems, out_sems,
):
    freqs, _, width, depth = left.shape
    count = freqs // 2
    half = width // 2
    rows = 2 * count
    tail = 2 * rows * BLOCK
    core, zi = lax.axis_index("core"), lax.axis_index("z")
    lane = lax.broadcasted_iota(jnp.int32, (BLOCK, LANES), 1)
    level = lax.broadcasted_iota(jnp.int32, (BLOCK, LANES), 0)

    def fetch_left(i):
        return pltpu.make_async_copy(spectra.at[i], left.at[i], left_sems.at[i])

    def fetch_right(i):
        return pltpu.make_async_copy(primaries.at[i], right.at[i], right_sems.at[i])

    for i in range(freqs):
        fetch_right(i).start()
        fetch_left(i).start()
    block = lax.broadcasted_iota(jnp.int32, (8, width), 1) // BLOCK
    source = jnp.zeros((8, width), jnp.int32)
    for b in range(width // BLOCK):
        source = jnp.where(block == b, pairing[b], source)
    source = source * BLOCK + lax.broadcasted_iota(jnp.int32, (8, width), 1) % BLOCK
    for r in range(0, width, 8):
        row = lax.broadcasted_iota(jnp.int32, (8, width), 0) + r
        relabel[r : r + 8] = jnp.where(row == source, 1.0, 0.0)
    relabel_low[...] = relabel[...].astype(jnp.bfloat16)
    out[:, tail:] = jnp.zeros((out.shape[0], out.shape[1] - tail, LANES), out.dtype)
    for second in range(2):
        long_up = second == core
        for t in range(RING):
            k = lax.rem(t - zi + RING, RING)
            away = jnp.where(k <= 4, 4 - k, k - 4)
            goes_up = (k < 4) | ((k == 4) & long_up)
            send = 2 * away - jnp.where(long_up == goes_up, 0, 1)
            mine = goes_up == (core == 0)
            slots[second, t] = jnp.where(k == 0, 14 + second, send + jnp.where(mine, 0, 7))

    def cut(i):
        second = lax.div(i, count)
        real, imag = held[i & 1, 0], held[i & 1, 1]
        real = 0.5 * (real + real.T)
        imag = 0.5 * (imag + imag.T)
        wr = ratio[0, i]
        wi = ratio[1, i]
        for c, z in enumerate((wr * real - wi * imag, wr * imag + wi * real)):
            row = 2 * i + c
            shift = row & 7
            place = tail + (row >> 3) - second * (2 * count // 8)
            row = row - second * rows
            for t in range(RING):
                k = slots[second, t]
                low = z[BLOCK * t : BLOCK * (t + 1)]
                high = z[half + BLOCK * t : half + BLOCK * (t + 1)]
                out[k, pl.ds(pl.multiple_of(row * BLOCK, BLOCK), BLOCK)] = window(
                    low[:, :half], low[:, half:], BLOCK * t
                )
                out[k, pl.ds(pl.multiple_of((rows + row) * BLOCK, BLOCK), BLOCK)] = window(
                    high[:, half:], high[:, :half], BLOCK * t
                )
                middle = jnp.where(lane == level + BLOCK * t, low[:, half:], 0.0)
                middle = jnp.sum(middle, axis=0, keepdims=True)
                middle = pltpu.roll(middle, (BLOCK * (shift - t)) & (LANES - 1), 1)
                out[k, pl.ds(place, 1)] += middle

    def multiply(i):
        a = left[i].reshape(2 * width, depth)
        by_real = jnp.dot(a, chosen[i & 1, 0], preferred_element_type=jnp.float32)
        by_imag = jnp.dot(a, chosen[i & 1, 1], preferred_element_type=jnp.float32)
        held[i & 1, 0] = by_real[:width] - by_imag[width:]
        held[i & 1, 1] = by_imag[:width] + by_real[width:]

    def choose(i):
        for b in range(2):
            chosen[i & 1, b] = jnp.dot(
                right[i, b], relabel_low[...], preferred_element_type=jnp.float32
            ).astype(jnp.bfloat16)

    def stages(i, carry):
        fetch_right(i).wait()
        fetch_left(i - 1).wait()
        cut(i - 2)
        multiply(i - 1)
        choose(i)
        return carry

    def copies(moves):
        return [
            pltpu.make_async_copy(out.at[slot], dst.at[i], out_sems.at[slot])
            for slot, dst, i in moves
        ]

    def unit(first, some, last, n):
        return (first, 0) if n == 0 else (some, n - 1) if n < 4 else (last, n - 4)

    moves = [(n,) + unit(keep_first, keep, keep_last, n) for n in range(7)]
    moves += [(7 + n,) + unit(give_first, give, give_last, n) for n in range(7)]
    early = copies([moves[n] for n in (0, 2, 4, 6, 8, 10, 12)] + [(14, own, 0)])
    late = copies([moves[n] for n in (7, 1, 3, 5, 9, 11, 13)] + [(15, own, 1)])
    fetch_right(0).wait()
    choose(0)
    fetch_right(1).wait()
    fetch_left(0).wait()
    multiply(0)
    choose(1)
    lax.fori_loop(2, count + 2, stages, 0)
    for copy in early:
        copy.start()
    lax.fori_loop(count + 2, freqs, stages, 0)
    fetch_left(freqs - 1).wait()
    cut(freqs - 2)
    multiply(freqs - 1)
    cut(freqs - 1)
    for copy in late:
        copy.start()
    for copy in early + late:
        copy.wait()


def product(spectra, primaries, ratio, pairing):
    freqs = spectra.shape[0]
    width, depth = spectra.shape[2:]
    height = 2 * freqs * BLOCK + 8
    smem = pl.BlockSpec(memory_space=pltpu.SMEM)
    anywhere = pl.BlockSpec(memory_space=pl.ANY)
    shapes = [(n, height, LANES) for n in (1, 3, 3, 1, 3, 3, 2)]
    return pl.pallas_call(
        product_kernel,
        in_specs=[smem, smem, anywhere, anywhere],
        out_specs=[anywhere] * 7,
        out_shape=[jax.ShapeDtypeStruct(s, jnp.float32) for s in shapes],
        scratch_shapes=[
            pltpu.VMEM(spectra.shape, spectra.dtype),
            pltpu.VMEM(primaries.shape, primaries.dtype),
            pltpu.VMEM((width, width), jnp.float32),
            pltpu.VMEM((width, width), jnp.bfloat16),
            pltpu.VMEM((2, 2, depth, width), jnp.bfloat16),
            pltpu.VMEM((2, 2, width, width), jnp.float32),
            pltpu.VMEM((16, height, LANES), jnp.float32),
            pltpu.SMEM((2, RING), jnp.int32),
            pltpu.SemaphoreType.DMA((freqs,)),
            pltpu.SemaphoreType.DMA((freqs,)),
            pltpu.SemaphoreType.DMA((16,)),
        ],
        compiler_params=pltpu.CompilerParams(vmem_limit_bytes=PRODUCT_VMEM),
        cost_estimate=pl.CostEstimate(
            flops=freqs * 2 * 2 * width * 2 * width * depth,
            bytes_accessed=freqs * 8 * width * depth + 16 * height * LANES * 4,
            transcendentals=0,
        ),
        name="product",
    )(pairing, ratio, spectra, primaries)


def collect_kernel(arrivals, keep, got, *refs):
    arrived, outs = refs[:arrivals], refs[arrivals + 1 :]
    outs = outs if len(outs) == 2 else (outs[0].at[pl.ds(0, 1)], outs[0].at[pl.ds(1, 1)])
    for i, part in enumerate((keep, got)):
        outs[i][0] = arrived[0][i] + part[0] if arrived else part[0]


def collect(index, keep, got, before, *arrived, split=False):
    shape = (2,) + keep.shape[1:]
    one = pl.BlockSpec((1,) + shape[1:], lambda i: (index, 0, 0))
    whole = pl.BlockSpec(shape, lambda i: (0, 0, 0))
    half = pl.BlockSpec((1,) + shape[1:], lambda i: (0, 0, 0))
    return pl.pallas_call(
        functools.partial(collect_kernel, len(arrived)),
        grid=(1,),
        in_specs=[one, one] + [whole] * len(arrived) + [pl.BlockSpec(memory_space=pl.ANY)],
        out_specs=[half, half] if split else whole,
        out_shape=[jax.ShapeDtypeStruct((1,) + shape[1:], jnp.float32)] * 2
        if split
        else jax.ShapeDtypeStruct(shape, jnp.float32),
        compiler_params=pltpu.CompilerParams(vmem_limit_bytes=SMALL_VMEM),
        name="collect",
    )(keep, got, *arrived, before)


def exchange_lanes(tiles):
    lane = lax.broadcasted_iota(jnp.int32, tiles[0].shape, 1) // BLOCK
    for bit in (1, 2, 4):
        upper = (lane // bit) % 2 == 1
        out = list(tiles)
        for a in range(8):
            if a & bit:
                continue
            x, y = tiles[a], tiles[a | bit]
            if bit == 4:
                moved = pltpu.roll(jnp.where(upper, x, y), LANES // 2, 1)
                out[a], out[a | bit] = jnp.where(upper, moved, x), jnp.where(upper, y, moved)
                continue
            out[a] = jnp.where(upper, pltpu.roll(y, BLOCK * bit, 1), x)
            out[a | bit] = jnp.where(upper, y, pltpu.roll(x, LANES - BLOCK * bit, 1))
        tiles = out
    return tiles


def ring_total(refs, half, start, size=BLOCK):
    own, late, early, got_late, got_early = refs
    at = pl.ds(start, size)
    if half:
        return own[1, at] + early[0, at] + got_late[at]
    return own[0, at] + late[0, at] + got_early[at]


def direct_kernel(*refs):
    keep, give = refs[6:]
    yl = lax.axis_index("yl")
    rows = keep.shape[0] // 2
    for half in range(2):
        for a in range(rows):
            for h, dst in ((yl, keep), (1 - yl, give)):
                start = pl.multiple_of(BLOCK * (rows * h + a), BLOCK)
                dst[rows * half + a] = ring_total(refs[:5], half, start)


def mail_kernel(*refs):
    mail = refs[5]
    zi = lax.axis_index("z")
    groups = mail.shape[1]
    rows = 4 * groups
    across = lax.broadcasted_iota(jnp.int32, (BLOCK, LANES), 1) % BLOCK
    down = lax.broadcasted_iota(jnp.int32, (BLOCK, LANES), 0)

    for g in range(groups):
        firsts = []
        for h in range(2):
            tiles = [
                ring_total(refs[:5], row // rows, BLOCK * (rows * h + row % rows))
                for row in range(8 * g, 8 * g + 8)
            ]
            swapped = exchange_lanes(tiles)
            firsts.append(swapped[0])
            for m in range(1, 8):
                mail[lax.rem(zi + 8 * h + m, 16), g] = swapped[m]
        middle = 0.0
        for half in range(2):
            if rows * half < 8 * g + 8 and rows * (half + 1) > 8 * g:
                place = 2 * rows * BLOCK + g - rows * half // 8
                middle = middle + ring_total(refs[:5], half, place, 1)
        for at, below in ((8, firsts[0]), (0, firsts[1])):
            mail[zi + at, g] = jnp.where(across == down, middle, below)


def pack(rows, *sums):
    whole = pl.BlockSpec(memory_space=pltpu.VMEM)

    def call(kernel, shapes, name, *before):
        return pl.pallas_call(
            kernel,
            in_specs=[whole] * 5 + [pl.BlockSpec(memory_space=pl.ANY)] * len(before),
            out_specs=[whole] * len(shapes),
            out_shape=[jax.ShapeDtypeStruct(s, jnp.float32) for s in shapes],
            compiler_params=pltpu.CompilerParams(vmem_limit_bytes=SMALL_VMEM),
            name=name,
        )(*sums, *before)

    (mail,) = call(mail_kernel, [(16, rows // 8, BLOCK, LANES)], "mail")
    keep, give = call(direct_kernel, [(rows, BLOCK, LANES)] * 2, "direct", mail)
    return keep, give, mail


def join_kernel(keep, got, mail, out):
    zi = lax.axis_index("z")
    groups = mail.shape[1]
    lane = lax.broadcasted_iota(jnp.int32, (BLOCK, LANES), 1)
    level = lax.broadcasted_iota(jnp.int32, (BLOCK, LANES), 0)
    rest = jnp.zeros((BLOCK, LANES - BLOCK), jnp.float32)
    for g in range(groups):
        stack = []
        for k in range(8):
            z = lax.rem(zi + k, 8)
            stack.append(mail[z, g] + mail[z + 8, g])
        turned = jnp.concatenate(stack, axis=0).T.reshape(8, BLOCK, LANES)
        tiles = [keep[8 * g + a] + got[8 * g + a] for a in range(8)]
        packed = jnp.where(lane < BLOCK, tiles[0], 0.0)
        for a in range(1, 8):
            packed = packed + pltpu.roll(jnp.where(lane < BLOCK, tiles[a], 0.0), BLOCK * a, 1)
        upper = packed.T
        own = lane < level
        direct = [
            jnp.where(
                own, jnp.concatenate([upper[BLOCK * a : BLOCK * (a + 1)], rest], axis=1), tiles[a]
            )
            for a in range(8)
        ]
        mirrored = [jnp.where(own, tiles[a], turned[a]) for a in range(8)]
        out[:, 8 * g : 8 * g + 8, :LANES] = jnp.swapaxes(jnp.stack(direct), 0, 1)
        out[:, 8 * g : 8 * g + 8, LANES:] = jnp.swapaxes(jnp.stack(mirrored), 0, 1)


def join(keep, got, mail):
    groups = mail.shape[1]
    whole = pl.BlockSpec(memory_space=pltpu.VMEM)
    return pl.pallas_call(
        join_kernel,
        in_specs=[whole] * 3,
        out_specs=whole,
        out_shape=jax.ShapeDtypeStruct((BLOCK, 8 * groups, 2 * LANES), jnp.float32),
        compiler_params=pltpu.CompilerParams(vmem_limit_bytes=SMALL_VMEM),
        name="join",
    )(keep, got, mail)


def transform_kernel(basis, data, relabel, out):
    dot = functools.partial(jnp.dot, preferred_element_type=jnp.float32)
    x = data[...]
    high = x.astype(jnp.bfloat16)
    low = (x - high.astype(jnp.float32)).astype(jnp.bfloat16)
    high = dot(high, relabel[...]).astype(jnp.bfloat16)
    low = dot(low, relabel[...]).astype(jnp.bfloat16)
    out[...] = dot(basis[0], high) + (dot(basis[0], low) + dot(basis[1], high))


def transform(basis, data, relabel):
    whole = pl.BlockSpec(memory_space=pltpu.VMEM)
    return pl.pallas_call(
        transform_kernel,
        in_specs=[whole] * 3,
        out_specs=whole,
        out_shape=jax.ShapeDtypeStruct((basis.shape[1], data.shape[1]), jnp.float32),
        compiler_params=pltpu.CompilerParams(vmem_limit_bytes=SMALL_VMEM),
        name="transform",
    )(basis, data, relabel)


def update_kernel(events, inside, traces, older, data, out):
    count = older.shape[0]
    for t in range(count):
        old = older[t].astype(jnp.float32)
        moved = old + step_weight * events[t] * (
            data[t].astype(jnp.float32) - old - traces[:, t, :]
        )
        size = jnp.maximum(jnp.abs(moved) - shrink_level, 0.0)
        shrunk = jnp.where(moved < 0.0, -size, size)
        out[t] = jnp.where(inside[t] > 0, shrunk, 0.0).astype(jnp.bfloat16)


def update(events, inside, traces, older, data):
    whole = pl.BlockSpec(memory_space=pltpu.VMEM)
    scalars = pl.BlockSpec(memory_space=pltpu.SMEM)
    return pl.pallas_call(
        update_kernel,
        in_specs=[scalars, scalars, whole, whole, whole],
        out_specs=whole,
        out_shape=jax.ShapeDtypeStruct(older.shape, jnp.bfloat16),
        compiler_params=pltpu.CompilerParams(vmem_limit_bytes=SMALL_VMEM),
        name="update",
    )(events, inside, traces, older, data)


def slot_windows(slots, window_lengths, capacity):
    starts = jnp.cumsum(window_lengths) - window_lengths
    window = slots // capacity
    offset = slots % capacity
    select = window[:, None] == jnp.arange(window_lengths.shape[0], dtype=jnp.int32)[None, :]
    begin = jnp.sum(jnp.where(select, starts[None, :], 0), axis=1)
    length = jnp.sum(jnp.where(select, window_lengths[None, :], 0), axis=1)
    return begin + offset, offset < length


def time_basis(times, inside, freqs):
    phase = times[:, None] * freqs[None, :] % NT
    angle = phase.astype(jnp.float32) * (2.0 * math.pi / NT)
    scale = jnp.where(inside, 1.0 / math.sqrt(F), 0.0).astype(jnp.float32)[:, None]
    odd = (jnp.arange(freqs.shape[0]) % 2 == 1)[None, :]
    return jnp.where(odd, -jnp.sin(angle), jnp.cos(angle)) * scale


def ring(n, d):
    return [(i, (i + d) % n) for i in range(n)]


def other_half_kernel(arrived, before, out):
    out[...] = arrived[1]


def other_half(arrived, before):
    whole = pl.BlockSpec(memory_space=pltpu.VMEM)
    return pl.pallas_call(
        other_half_kernel,
        in_specs=[whole, pl.BlockSpec(memory_space=pl.ANY)],
        out_specs=whole,
        out_shape=jax.ShapeDtypeStruct(arrived.shape[1:], arrived.dtype),
        compiler_params=pltpu.CompilerParams(vmem_limit_bytes=SMALL_VMEM),
        name="other_half",
    )(arrived, before)


def lift_kernel(source, out, sem):
    copy = pltpu.make_async_copy(source, out, sem)
    copy.start()
    copy.wait()


def lift(source):
    return pl.pallas_call(
        lift_kernel,
        in_specs=[pl.BlockSpec(memory_space=pl.ANY)],
        out_specs=pl.BlockSpec(memory_space=pltpu.VMEM),
        out_shape=jax.ShapeDtypeStruct(source.shape, source.dtype),
        scratch_shapes=[pltpu.SemaphoreType.DMA],
        compiler_params=pltpu.CompilerParams(vmem_limit_bytes=SMALL_VMEM),
        cost_estimate=pl.CostEstimate(
            flops=0, bytes_accessed=8 * source.size, transcendentals=0
        ),
        name="lift",
    )(source)


def ring_sums(keep_first, keep, keep_last, give_first, give, give_last):
    swap = functools.partial(lax.ppermute, axis_name="core", perm=ring(2, 1))
    step = functools.partial(
        lax.ppermute,
        axis_name=("core", "z"),
        perm=[
            (c * RING + z, c * RING + (z + (1 if c == 0 else -1)) % RING)
            for c in range(2)
            for z in range(RING)
        ],
    )
    cross = functools.partial(
        lax.ppermute,
        axis_name=("core", "z"),
        perm=[
            (c * RING + z, (1 - c) * RING + (z + (1 if c == 0 else -1)) % RING)
            for c in range(2)
            for z in range(RING)
        ],
    )
    payload = collect(0, lift(keep_first), swap(give_first), keep_first)
    payload, give = lax.optimization_barrier((payload, give))
    got = swap(give)
    flying = [step(payload)]
    for n in range(5):
        if n == 1:
            payload, give_last = lax.optimization_barrier((payload, give_last))
            got_last = swap(give_last)
        if n == 3:
            keep, got = keep_last, got_last
        payload = collect(n % 3, keep, got, payload, *flying[:-1])
        flying = flying[-1:] + [step(payload)]
    mine, other = collect(2, keep, got, payload, flying[0], split=True)
    return step(mine), flying[1], cross(other)[0], swap(other_half(flying[1], other))


def on_device(
    spectra, primaries, wavelet_ratio, window_lengths, event_mask, pairing, old_traces, data_traces
):
    src = ("yl", "z")
    freq = ("x", "yh", "core")
    freq_count = lax.axis_size(freq)
    freq_dev = spectra.shape[0]
    width = spectra.shape[2]
    capacity = old_traces.shape[0]
    yl, zi = lax.axis_index("yl"), lax.axis_index("z")
    own = yl * 8 + zi
    lanes = jnp.arange(width, dtype=jnp.int32)
    blocks = lanes // BLOCK
    ids = jnp.arange(pairing.shape[0], dtype=jnp.int32)

    def paired(block):
        return jnp.sum(jnp.where(block[:, None] == ids[None, :], pairing[None, :], 0), axis=1)

    target = paired((blocks + own) % pairing.shape[0]) * BLOCK + lanes % BLOCK
    restore = (target[:, None] == lanes[None, :]).astype(jnp.bfloat16)
    slots = jnp.arange(capacity * freq_count, dtype=jnp.int32)
    times, inside = slot_windows(slots, window_lengths, capacity)
    basis = time_basis(
        times, inside, jnp.arange(2 * freq_dev * freq_count, dtype=jnp.int32) // 2
    )
    coarse = lax.reduce_precision(basis, 8, 7)
    basis = jnp.stack([coarse, basis - coarse]).astype(jnp.bfloat16)
    own_slots = lax.axis_index(freq) * capacity + jnp.arange(capacity, dtype=jnp.int32)
    _, inside_own = slot_windows(own_slots, window_lengths, capacity)

    *sends, ends = product(spectra, primaries, wavelet_ratio, pairing)
    keep, give, mail = pack(2 * freq_dev, ends, *ring_sums(*sends))
    got = lax.ppermute(give, "yl", ring(2, 1))
    mail = lax.all_to_all(mail, src, split_axis=0, concat_axis=0, tiled=True)
    whole = join(keep, got, mail)
    spread = lax.all_to_all(whole, freq, split_axis=0, concat_axis=0, tiled=True)
    slotted = transform(basis, spread.reshape(-1, width), restore)
    slotted = slotted.reshape(freq_count, capacity, width)
    traces = lax.all_to_all(slotted, freq, split_axis=0, concat_axis=0, tiled=True)
    return update(
        event_mask.astype(jnp.float32),
        inside_own.astype(jnp.int32),
        traces,
        old_traces,
        data_traces,
    )


def solution(mesh):
    shape = tuple(mesh.shape.values())
    cores = 2 if shape[0] % 2 == 0 else 1
    yh = 2 if shape[0] % 4 == 0 else 1
    devices = mesh.devices.reshape(shape[0] // (cores * yh), yh, cores, shape[1] // 8, 8)
    split = Mesh(devices, ("x", "yh", "core", "yl", "z"))
    freq = ("x", "yh", "core")
    src = ("yl", "z")
    in_specs = (
        P(freq, None, None, src),
        P(freq, None, src, None),
        P(None, freq),
        P(),
        P(freq),
        P(),
        P(freq, src, None),
        P(freq, src, None),
    )
    return jax.shard_map(
        on_device, mesh=split, in_specs=in_specs, out_specs=P(freq, src, None), check_vma=False
    )
```

```python
import functools
import math

import jax
import jax.numpy as jnp
from jax import lax
from jax.experimental import pallas as pl
from jax.experimental.pallas import tpu as pltpu
from jax.sharding import Mesh, PartitionSpec as P

F = 192
NT = 384
LANES = 128
BLOCK = 16
RING = 8
PRODUCT_VMEM = 59 * 1024 * 1024
SMALL_VMEM = 24 * 1024 * 1024

shrink_level = 0.25
step_weight = 0.5


def window(near, far, shift):
    lane = lax.broadcasted_iota(jnp.int32, near.shape, 1)
    row = lax.broadcasted_iota(jnp.int32, near.shape, 0)
    if shift:
        near = pltpu.roll(near, LANES - shift, 1)
        far = pltpu.roll(far, LANES - shift, 1)
    return jnp.where((lane < LANES - shift) & (lane >= row), near, far)


def product_kernel(
    pairing, ratio, spectra, primaries, keep_first, keep, keep_last, give_first, give, give_last, own,
    left, right, relabel, relabel_low, chosen, held, out, slots, left_sems, right_sems, out_sems,
):
    freqs, _, width, depth = left.shape
    count = freqs // 2
    half = width // 2
    rows = 2 * count
    tail = 2 * rows * BLOCK
    core, zi = lax.axis_index("core"), lax.axis_index("z")
    lane = lax.broadcasted_iota(jnp.int32, (BLOCK, LANES), 1)
    level = lax.broadcasted_iota(jnp.int32, (BLOCK, LANES), 0)

    def fetch_left(i):
        return pltpu.make_async_copy(spectra.at[i], left.at[i], left_sems.at[i])

    def fetch_right(i):
        return pltpu.make_async_copy(primaries.at[i], right.at[i], right_sems.at[i])

    for i in range(freqs):
        fetch_right(i).start()
        fetch_left(i).start()
    block = lax.broadcasted_iota(jnp.int32, (8, width), 1) // BLOCK
    source = jnp.zeros((8, width), jnp.int32)
    for b in range(width // BLOCK):
        source = jnp.where(block == b, pairing[b], source)
    source = source * BLOCK + lax.broadcasted_iota(jnp.int32, (8, width), 1) % BLOCK
    for r in range(0, width, 8):
        row = lax.broadcasted_iota(jnp.int32, (8, width), 0) + r
        relabel[r : r + 8] = jnp.where(row == source, 1.0, 0.0)
    relabel_low[...] = relabel[...].astype(jnp.bfloat16)
    out[:, tail:] = jnp.zeros((out.shape[0], out.shape[1] - tail, LANES), out.dtype)
    for second in range(2):
        long_up = second == core
        for t in range(RING):
            k = lax.rem(t - zi + RING, RING)
            away = jnp.where(k <= 4, 4 - k, k - 4)
            goes_up = (k < 4) | ((k == 4) & long_up)
            send = 2 * away - jnp.where(long_up == goes_up, 0, 1)
            mine = goes_up == (core == 0)
            slots[second, t] = jnp.where(k == 0, 14 + second, send + jnp.where(mine, 0, 7))

    def cut(i):
        second = lax.div(i, count)
        real, imag = held[i & 1, 0], held[i & 1, 1]
        real = 0.5 * (real + real.T)
        imag = 0.5 * (imag + imag.T)
        wr = ratio[0, i]
        wi = ratio[1, i]
        for c, z in enumerate((wr * real - wi * imag, wr * imag + wi * real)):
            row = 2 * i + c
            shift = row & 7
            place = tail + (row >> 3) - second * (2 * count // 8)
            row = row - second * rows
            for t in range(RING):
                k = slots[second, t]
                low = z[BLOCK * t : BLOCK * (t + 1)]
                high = z[half + BLOCK * t : half + BLOCK * (t + 1)]
                out[k, pl.ds(pl.multiple_of(row * BLOCK, BLOCK), BLOCK)] = window(
                    low[:, :half], low[:, half:], BLOCK * t
                )
                out[k, pl.ds(pl.multiple_of((rows + row) * BLOCK, BLOCK), BLOCK)] = window(
                    high[:, half:], high[:, :half], BLOCK * t
                )
                middle = jnp.where(lane == level + BLOCK * t, low[:, half:], 0.0)
                middle = jnp.sum(middle, axis=0, keepdims=True)
                middle = pltpu.roll(middle, (BLOCK * (shift - t)) & (LANES - 1), 1)
                out[k, pl.ds(place, 1)] += middle

    def multiply(i):
        a = left[i].reshape(2 * width, depth)
        by_real = jnp.dot(a, chosen[i & 1, 0], preferred_element_type=jnp.float32)
        by_imag = jnp.dot(a, chosen[i & 1, 1], preferred_element_type=jnp.float32)
        held[i & 1, 0] = by_real[:width] - by_imag[width:]
        held[i & 1, 1] = by_imag[:width] + by_real[width:]

    def choose(i):
        for b in range(2):
            chosen[i & 1, b] = jnp.dot(
                right[i, b], relabel_low[...], preferred_element_type=jnp.float32
            ).astype(jnp.bfloat16)

    def stages(i, carry):
        fetch_right(i).wait()
        fetch_left(i - 1).wait()
        cut(i - 2)
        multiply(i - 1)
        choose(i)
        return carry

    def copies(moves):
        return [
            pltpu.make_async_copy(out.at[slot], dst.at[i], out_sems.at[slot])
            for slot, dst, i in moves
        ]

    def unit(first, some, last, n):
        return (first, 0) if n == 0 else (some, n - 1) if n < 4 else (last, n - 4)

    moves = [(n,) + unit(keep_first, keep, keep_last, n) for n in range(7)]
    moves += [(7 + n,) + unit(give_first, give, give_last, n) for n in range(7)]
    early = copies([moves[n] for n in (0, 2, 4, 6, 8, 10, 12)] + [(14, own, 0)])
    late = copies([moves[n] for n in (7, 1, 3, 5, 9, 11, 13)] + [(15, own, 1)])
    fetch_right(0).wait()
    choose(0)
    fetch_right(1).wait()
    fetch_left(0).wait()
    multiply(0)
    choose(1)
    lax.fori_loop(2, count + 2, stages, 0)
    for copy in early:
        copy.start()
    lax.fori_loop(count + 2, freqs, stages, 0)
    fetch_left(freqs - 1).wait()
    cut(freqs - 2)
    multiply(freqs - 1)
    cut(freqs - 1)
    for copy in late:
        copy.start()
    for copy in early + late:
        copy.wait()


def product(spectra, primaries, ratio, pairing):
    freqs = spectra.shape[0]
    width, depth = spectra.shape[2:]
    height = 2 * freqs * BLOCK + 8
    smem = pl.BlockSpec(memory_space=pltpu.SMEM)
    anywhere = pl.BlockSpec(memory_space=pl.ANY)
    shapes = [(n, height, LANES) for n in (1, 3, 3, 1, 3, 3, 2)]
    return pl.pallas_call(
        product_kernel,
        in_specs=[smem, smem, anywhere, anywhere],
        out_specs=[anywhere] * 7,
        out_shape=[jax.ShapeDtypeStruct(s, jnp.float32) for s in shapes],
        scratch_shapes=[
            pltpu.VMEM(spectra.shape, spectra.dtype),
            pltpu.VMEM(primaries.shape, primaries.dtype),
            pltpu.VMEM((width, width), jnp.float32),
            pltpu.VMEM((width, width), jnp.bfloat16),
            pltpu.VMEM((2, 2, depth, width), jnp.bfloat16),
            pltpu.VMEM((2, 2, width, width), jnp.float32),
            pltpu.VMEM((16, height, LANES), jnp.float32),
            pltpu.SMEM((2, RING), jnp.int32),
            pltpu.SemaphoreType.DMA((freqs,)),
            pltpu.SemaphoreType.DMA((freqs,)),
            pltpu.SemaphoreType.DMA((16,)),
        ],
        compiler_params=pltpu.CompilerParams(vmem_limit_bytes=PRODUCT_VMEM),
        cost_estimate=pl.CostEstimate(
            flops=freqs * 2 * 2 * width * 2 * width * depth,
            bytes_accessed=freqs * 8 * width * depth + 16 * height * LANES * 4,
            transcendentals=0,
        ),
        name="product",
    )(pairing, ratio, spectra, primaries)


def collect_kernel(arrivals, keep, got, *refs):
    arrived, outs = refs[:arrivals], refs[arrivals + 1 :]
    outs = outs if len(outs) == 2 else (outs[0].at[pl.ds(0, 1)], outs[0].at[pl.ds(1, 1)])
    for i, part in enumerate((keep, got)):
        outs[i][0] = arrived[0][i] + part[0] if arrived else part[0]


def collect(index, keep, got, before, *arrived, split=False):
    shape = (2,) + keep.shape[1:]
    one = pl.BlockSpec((1,) + shape[1:], lambda i: (index, 0, 0))
    whole = pl.BlockSpec(shape, lambda i: (0, 0, 0))
    half = pl.BlockSpec((1,) + shape[1:], lambda i: (0, 0, 0))
    return pl.pallas_call(
        functools.partial(collect_kernel, len(arrived)),
        grid=(1,),
        in_specs=[one, one] + [whole] * len(arrived) + [pl.BlockSpec(memory_space=pl.ANY)],
        out_specs=[half, half] if split else whole,
        out_shape=[jax.ShapeDtypeStruct((1,) + shape[1:], jnp.float32)] * 2
        if split
        else jax.ShapeDtypeStruct(shape, jnp.float32),
        compiler_params=pltpu.CompilerParams(vmem_limit_bytes=SMALL_VMEM),
        name="collect",
    )(keep, got, *arrived, before)


def exchange_lanes(tiles):
    lane = lax.broadcasted_iota(jnp.int32, tiles[0].shape, 1) // BLOCK
    for bit in (1, 2, 4):
        upper = (lane // bit) % 2 == 1
        out = list(tiles)
        for a in range(8):
            if a & bit:
                continue
            x, y = tiles[a], tiles[a | bit]
            if bit == 4:
                moved = pltpu.roll(jnp.where(upper, x, y), LANES // 2, 1)
                out[a], out[a | bit] = jnp.where(upper, moved, x), jnp.where(upper, y, moved)
                continue
            out[a] = jnp.where(upper, pltpu.roll(y, BLOCK * bit, 1), x)
            out[a | bit] = jnp.where(upper, y, pltpu.roll(x, LANES - BLOCK * bit, 1))
        tiles = out
    return tiles


def ring_total(refs, half, start, size=BLOCK):
    own, late, early, got_late, got_early = refs
    at = pl.ds(start, size)
    if half:
        return own[1, at] + early[0, at] + got_late[at]
    return own[0, at] + late[0, at] + got_early[at]


def direct_kernel(*refs):
    keep, give = refs[6:]
    yl = lax.axis_index("yl")
    rows = keep.shape[0] // 2
    for half in range(2):
        for a in range(rows):
            for h, dst in ((yl, keep), (1 - yl, give)):
                start = pl.multiple_of(BLOCK * (rows * h + a), BLOCK)
                dst[rows * half + a] = ring_total(refs[:5], half, start)


def mail_kernel(*refs):
    mail = refs[5]
    zi = lax.axis_index("z")
    groups = mail.shape[1]
    rows = 4 * groups
    across = lax.broadcasted_iota(jnp.int32, (BLOCK, LANES), 1) % BLOCK
    down = lax.broadcasted_iota(jnp.int32, (BLOCK, LANES), 0)

    for g in range(groups):
        firsts = []
        for h in range(2):
            tiles = [
                ring_total(refs[:5], row // rows, BLOCK * (rows * h + row % rows))
                for row in range(8 * g, 8 * g + 8)
            ]
            swapped = exchange_lanes(tiles)
            firsts.append(swapped[0])
            for m in range(1, 8):
                mail[lax.rem(zi + 8 * h + m, 16), g] = swapped[m]
        middle = 0.0
        for half in range(2):
            if rows * half < 8 * g + 8 and rows * (half + 1) > 8 * g:
                place = 2 * rows * BLOCK + g - rows * half // 8
                middle = middle + ring_total(refs[:5], half, place, 1)
        for at, below in ((8, firsts[0]), (0, firsts[1])):
            mail[zi + at, g] = jnp.where(across == down, middle, below)


def pack(rows, *sums):
    whole = pl.BlockSpec(memory_space=pltpu.VMEM)

    def call(kernel, shapes, name, *before):
        return pl.pallas_call(
            kernel,
            in_specs=[whole] * 5 + [pl.BlockSpec(memory_space=pl.ANY)] * len(before),
            out_specs=[whole] * len(shapes),
            out_shape=[jax.ShapeDtypeStruct(s, jnp.float32) for s in shapes],
            compiler_params=pltpu.CompilerParams(vmem_limit_bytes=SMALL_VMEM),
            name=name,
        )(*sums, *before)

    (mail,) = call(mail_kernel, [(16, rows // 8, BLOCK, LANES)], "mail")
    keep, give = call(direct_kernel, [(rows, BLOCK, LANES)] * 2, "direct", mail)
    return keep, give, mail


def join_kernel(keep, got, mail, out):
    zi = lax.axis_index("z")
    groups = mail.shape[1]
    lane = lax.broadcasted_iota(jnp.int32, (BLOCK, LANES), 1)
    level = lax.broadcasted_iota(jnp.int32, (BLOCK, LANES), 0)
    rest = jnp.zeros((BLOCK, LANES - BLOCK), jnp.float32)
    for g in range(groups):
        stack = []
        for k in range(8):
            z = lax.rem(zi + k, 8)
            stack.append(mail[z, g] + mail[z + 8, g])
        turned = jnp.concatenate(stack, axis=0).T.reshape(8, BLOCK, LANES)
        tiles = [keep[8 * g + a] + got[8 * g + a] for a in range(8)]
        packed = jnp.where(lane < BLOCK, tiles[0], 0.0)
        for a in range(1, 8):
            packed = packed + pltpu.roll(jnp.where(lane < BLOCK, tiles[a], 0.0), BLOCK * a, 1)
        upper = packed.T
        own = lane < level
        direct = [
            jnp.where(
                own, jnp.concatenate([upper[BLOCK * a : BLOCK * (a + 1)], rest], axis=1), tiles[a]
            )
            for a in range(8)
        ]
        mirrored = [jnp.where(own, tiles[a], turned[a]) for a in range(8)]
        out[:, 8 * g : 8 * g + 8, :LANES] = jnp.swapaxes(jnp.stack(direct), 0, 1)
        out[:, 8 * g : 8 * g + 8, LANES:] = jnp.swapaxes(jnp.stack(mirrored), 0, 1)


def join(keep, got, mail):
    groups = mail.shape[1]
    whole = pl.BlockSpec(memory_space=pltpu.VMEM)
    return pl.pallas_call(
        join_kernel,
        in_specs=[whole] * 3,
        out_specs=whole,
        out_shape=jax.ShapeDtypeStruct((BLOCK, 8 * groups, 2 * LANES), jnp.float32),
        compiler_params=pltpu.CompilerParams(vmem_limit_bytes=SMALL_VMEM),
        name="join",
    )(keep, got, mail)


def transform_kernel(basis, data, relabel, out):
    dot = functools.partial(jnp.dot, preferred_element_type=jnp.float32)
    x = data[...]
    high = x.astype(jnp.bfloat16)
    low = (x - high.astype(jnp.float32)).astype(jnp.bfloat16)
    high = dot(high, relabel[...]).astype(jnp.bfloat16)
    low = dot(low, relabel[...]).astype(jnp.bfloat16)
    out[...] = dot(basis[0], high) + (dot(basis[0], low) + dot(basis[1], high))


def transform(basis, data, relabel):
    whole = pl.BlockSpec(memory_space=pltpu.VMEM)
    return pl.pallas_call(
        transform_kernel,
        in_specs=[whole] * 3,
        out_specs=whole,
        out_shape=jax.ShapeDtypeStruct((basis.shape[1], data.shape[1]), jnp.float32),
        compiler_params=pltpu.CompilerParams(vmem_limit_bytes=SMALL_VMEM),
        name="transform",
    )(basis, data, relabel)


def update_kernel(events, inside, traces, older, data, out):
    count = older.shape[0]
    turned = jnp.swapaxes(traces[...], 0, 1)
    for t in range(count):
        old = older[t].astype(jnp.float32)
        moved = old + step_weight * events[t] * (
            data[t].astype(jnp.float32) - old - turned[t]
        )
        size = jnp.maximum(jnp.abs(moved) - shrink_level, 0.0)
        shrunk = jnp.where(moved < 0.0, -size, size)
        out[t] = jnp.where(inside[t] > 0, shrunk, 0.0).astype(jnp.bfloat16)


def update(events, inside, traces, older, data):
    whole = pl.BlockSpec(memory_space=pltpu.VMEM)
    scalars = pl.BlockSpec(memory_space=pltpu.SMEM)
    return pl.pallas_call(
        update_kernel,
        in_specs=[scalars, scalars, whole, whole, whole],
        out_specs=whole,
        out_shape=jax.ShapeDtypeStruct(older.shape, jnp.bfloat16),
        compiler_params=pltpu.CompilerParams(vmem_limit_bytes=SMALL_VMEM),
        name="update",
    )(events, inside, traces, older, data)


def slot_windows(slots, window_lengths, capacity):
    starts = jnp.cumsum(window_lengths) - window_lengths
    window = slots // capacity
    offset = slots % capacity
    select = window[:, None] == jnp.arange(window_lengths.shape[0], dtype=jnp.int32)[None, :]
    begin = jnp.sum(jnp.where(select, starts[None, :], 0), axis=1)
    length = jnp.sum(jnp.where(select, window_lengths[None, :], 0), axis=1)
    return begin + offset, offset < length


def time_basis(times, inside, freqs):
    phase = times[:, None] * freqs[None, :] % NT
    angle = phase.astype(jnp.float32) * (2.0 * math.pi / NT)
    scale = jnp.where(inside, 1.0 / math.sqrt(F), 0.0).astype(jnp.float32)[:, None]
    odd = (jnp.arange(freqs.shape[0]) % 2 == 1)[None, :]
    return jnp.where(odd, -jnp.sin(angle), jnp.cos(angle)) * scale


def ring(n, d):
    return [(i, (i + d) % n) for i in range(n)]


def other_half_kernel(arrived, before, out):
    out[...] = arrived[1]


def other_half(arrived, before):
    whole = pl.BlockSpec(memory_space=pltpu.VMEM)
    return pl.pallas_call(
        other_half_kernel,
        in_specs=[whole, pl.BlockSpec(memory_space=pl.ANY)],
        out_specs=whole,
        out_shape=jax.ShapeDtypeStruct(arrived.shape[1:], arrived.dtype),
        compiler_params=pltpu.CompilerParams(vmem_limit_bytes=SMALL_VMEM),
        name="other_half",
    )(arrived, before)


def lift_kernel(source, out, sem):
    copy = pltpu.make_async_copy(source, out, sem)
    copy.start()
    copy.wait()


def lift(source):
    return pl.pallas_call(
        lift_kernel,
        in_specs=[pl.BlockSpec(memory_space=pl.ANY)],
        out_specs=pl.BlockSpec(memory_space=pltpu.VMEM),
        out_shape=jax.ShapeDtypeStruct(source.shape, source.dtype),
        scratch_shapes=[pltpu.SemaphoreType.DMA],
        compiler_params=pltpu.CompilerParams(vmem_limit_bytes=SMALL_VMEM),
        cost_estimate=pl.CostEstimate(
            flops=0, bytes_accessed=8 * source.size, transcendentals=0
        ),
        name="lift",
    )(source)


def ring_sums(keep_first, keep, keep_last, give_first, give, give_last):
    swap = functools.partial(lax.ppermute, axis_name="core", perm=ring(2, 1))
    step = functools.partial(
        lax.ppermute,
        axis_name=("core", "z"),
        perm=[
            (c * RING + z, c * RING + (z + (1 if c == 0 else -1)) % RING)
            for c in range(2)
            for z in range(RING)
        ],
    )
    cross = functools.partial(
        lax.ppermute,
        axis_name=("core", "z"),
        perm=[
            (c * RING + z, (1 - c) * RING + (z + (1 if c == 0 else -1)) % RING)
            for c in range(2)
            for z in range(RING)
        ],
    )
    payload = collect(0, lift(keep_first), swap(give_first), keep_first)
    payload, give = lax.optimization_barrier((payload, give))
    got = swap(give)
    keep = lift(keep)
    flying = [step(payload)]
    for n in range(5):
        if n == 1:
            payload, give_last = lax.optimization_barrier((payload, give_last))
            got_last = swap(give_last)
        if n == 3:
            keep, got = keep_last, got_last
        payload = collect(n % 3, keep, got, payload, *flying[:-1])
        flying = flying[-1:] + [step(payload)]
    mine, other = collect(2, keep, got, payload, flying[0], split=True)
    return step(mine), flying[1], cross(other)[0], swap(other_half(flying[1], other))


def on_device(
    spectra, primaries, wavelet_ratio, window_lengths, event_mask, pairing, old_traces, data_traces
):
    src = ("yl", "z")
    freq = ("x", "yh", "core")
    freq_count = lax.axis_size(freq)
    freq_dev = spectra.shape[0]
    width = spectra.shape[2]
    capacity = old_traces.shape[0]
    yl, zi = lax.axis_index("yl"), lax.axis_index("z")
    own = yl * 8 + zi
    lanes = jnp.arange(width, dtype=jnp.int32)
    blocks = lanes // BLOCK
    ids = jnp.arange(pairing.shape[0], dtype=jnp.int32)

    def paired(block):
        return jnp.sum(jnp.where(block[:, None] == ids[None, :], pairing[None, :], 0), axis=1)

    target = paired((blocks + own) % pairing.shape[0]) * BLOCK + lanes % BLOCK
    restore = (target[:, None] == lanes[None, :]).astype(jnp.bfloat16)
    slots = jnp.arange(capacity * freq_count, dtype=jnp.int32)
    times, inside = slot_windows(slots, window_lengths, capacity)
    basis = time_basis(
        times, inside, jnp.arange(2 * freq_dev * freq_count, dtype=jnp.int32) // 2
    )
    coarse = lax.reduce_precision(basis, 8, 7)
    basis = jnp.stack([coarse, basis - coarse]).astype(jnp.bfloat16)
    own_slots = lax.axis_index(freq) * capacity + jnp.arange(capacity, dtype=jnp.int32)
    _, inside_own = slot_windows(own_slots, window_lengths, capacity)

    *sends, ends = product(spectra, primaries, wavelet_ratio, pairing)
    keep, give, mail = pack(2 * freq_dev, ends, *ring_sums(*sends))
    got = lax.ppermute(give, "yl", ring(2, 1))
    mail = lax.all_to_all(mail, src, split_axis=0, concat_axis=0, tiled=True)
    whole = join(keep, got, mail)
    spread = lax.all_to_all(whole, freq, split_axis=0, concat_axis=0, tiled=True)
    slotted = transform(basis, spread.reshape(-1, width), restore)
    slotted = slotted.reshape(freq_count, capacity, width)
    traces = lax.all_to_all(slotted, freq, split_axis=0, concat_axis=0, tiled=True)
    return update(
        event_mask.astype(jnp.float32),
        inside_own.astype(jnp.int32),
        traces,
        old_traces,
        data_traces,
    )


def solution(mesh):
    shape = tuple(mesh.shape.values())
    cores = 2 if shape[0] % 2 == 0 else 1
    yh = 2 if shape[0] % 4 == 0 else 1
    devices = mesh.devices.reshape(shape[0] // (cores * yh), yh, cores, shape[1] // 8, 8)
    split = Mesh(devices, ("x", "yh", "core", "yl", "z"))
    freq = ("x", "yh", "core")
    src = ("yl", "z")
    in_specs = (
        P(freq, None, None, src),
        P(freq, None, src, None),
        P(None, freq),
        P(),
        P(freq),
        P(),
        P(freq, src, None),
        P(freq, src, None),
    )
    return jax.shard_map(
        on_device, mesh=split, in_specs=in_specs, out_specs=P(freq, src, None), check_vma=False
    )
```
